32 devices in a mesh: grid: 8 (over y, x, core), sta: 4 (over z).
Axes of the slice: x: 2, y: 2, z: 4, core: 2. Of those that a mesh axis runs over, the one named last changes fastest.
Arguments:
- spectra: bfloat16 [64, 2, 6144], P(None, None, 'sta'), may hold values from -6 to 6
- lag_samples: int32 [8, 6144], P('grid', 'sta'), may hold values from 0 to 5999
- slowness: bfloat16 [8, 3, 6144], P('grid', None, 'sta'), may hold values from -3 to 3
- spread_taps: float32 [3, 17], replicated, may hold values from 0.02 to 0.2
Outputs:
- stacked: float32 [8, 32, 8, 128], P('grid')
- deblurred: float32 [8, 32, 8, 128], P('grid')
The draws below stay inside these ranges and needn't reach their ends.
All inputs are finite; a program needn't handle non-finite values.
Results may differ from the reference program's by a relative error of at most 0.0015.
Values may be sent and summed in bfloat16 or wider, within the bound.
No kernel may reach another device: no remote copies, remote signals or barrier semaphores. Data moves between devices by JAX's collectives and lax.ppermute only.
A program may use at most 64 MiB of HBM per device.

```python
import math
import jax
import jax.numpy as jnp
from jax import lax

STATIONS = 6144
FREQS = 64
F0 = 600
NT = 6000
TAPS = 17
HALF = 8
ITERS = 4
CX = 32
CY = 8
CZ = 128
TX = 8
TY = 1
TILES = 8


def with_ends(drawn, own_key, low, largest):
    extent = drawn.shape
    index_at = [jax.random.randint(jax.random.fold_in(own_key, axis), (), 0, extent[axis]) for axis in range(len(extent))]
    drawn = drawn.at[tuple(index_at)].set(low)
    longest = extent.index(max(extent))
    index_at[longest] = (index_at[longest] + 1) % extent[longest]
    return drawn.at[tuple(index_at)].set(largest)


def level_of(stream_key, dims, pieces, low, largest):
    factor_of, own = 1.0, jax.random.fold_in(stream_key, 6)
    for dim, parts in pieces:
        draws = jnp.exp(jax.random.uniform(jax.random.fold_in(own, dim), (parts,), jnp.float32, low / len(pieces), largest / len(pieces)))
        factor_of = factor_of * jnp.repeat(draws, dims[dim] // parts).reshape([-1 if axis == dim else 1 for axis in range(len(dims))])
    return factor_of


def centred(key, extent, width, limit, split=(), kind=jnp.bfloat16):
    values = jax.random.normal(key, extent, jnp.float32) * width
    if len(split) > 0:
        values = level_of(key, extent, split, -0.22, 0.18) * values
    return jnp.clip(values, min=-limit, max=limit).astype(kind)


def setup_inputs(seed: int = 0) -> dict:
    key_of = jax.random.split(jax.random.key(seed), 5)
    spectra = centred(key_of[0], (FREQS, 2, STATIONS), 1.0, 6.0, ((2, 4),))
    lag_samples = with_ends(jax.random.randint(key_of[1], (TILES, STATIONS), 0, NT), jax.random.fold_in(key_of[1], 1), 0, NT - 1).astype(jnp.int32)
    slowness = jnp.clip(jax.random.uniform(key_of[2], (TILES, 3, STATIONS), jnp.float32, -3.0, 3.0) * level_of(key_of[2], (TILES, 3, STATIONS), ((0, 8), (2, 4)), -0.4, 0.0), -3.0, 3.0).astype(jnp.bfloat16)
    spread_taps = jnp.clip(jnp.exp(jax.random.uniform(key_of[3], (3, TAPS), jnp.float32, math.log(0.02), math.log(0.2))), 0.02, 0.2)
    return dict(spectra=spectra, lag_samples=lag_samples, slowness=slowness, spread_taps=spread_taps)


TWO_PI = 2.0 * math.pi
BACKGROUND = 0.05


def align_rows(spectra, lag_row):
    bins = (F0 + jnp.arange(FREQS, dtype=jnp.int32)).astype(jnp.int32)
    cycles = (bins[:, None] * lag_row[None, :].astype(jnp.int32)) % NT
    turned = cycles.astype(jnp.float32) * (TWO_PI / NT)
    cosine = jnp.cos(turned)
    sine = jnp.sin(turned)
    real_in = spectra[:, 0, :].astype(jnp.float32)
    imag_in = spectra[:, 1, :].astype(jnp.float32)
    real_out = real_in * cosine + imag_in * sine
    imag_out = imag_in * cosine - real_in * sine
    return jnp.stack([real_out, imag_out], axis=1).astype(jnp.bfloat16)


def beam_freq(freq, aligned_row, slow_rows):
    omega = (F0 + freq).astype(jnp.float32) * (TWO_PI / NT)
    slow = slow_rows.astype(jnp.float32)
    x_coord = jnp.arange(CX, dtype=jnp.float32) - (CX - 1) / 2.0
    y_coord = jnp.arange(CY, dtype=jnp.float32) - (CY - 1) / 2.0
    z_coord = jnp.arange(CZ, dtype=jnp.float32) - (CZ - 1) / 2.0
    phase_x = (omega * slow[0])[None, :] * x_coord[:, None]
    phase_y = (omega * slow[1])[None, :] * y_coord[:, None]
    phase = phase_x[:, None, :] + phase_y[None, :, :]
    cosine = jnp.cos(phase)
    sine = jnp.sin(phase)
    real_in = aligned_row[0].astype(jnp.float32)[None, None, :]
    imag_in = aligned_row[1].astype(jnp.float32)[None, None, :]
    front_real = (real_in * cosine + imag_in * sine).astype(jnp.bfloat16).reshape(CX * CY, -1)
    front_imag = (imag_in * cosine - real_in * sine).astype(jnp.bfloat16).reshape(CX * CY, -1)
    left_side = jnp.concatenate([front_real, front_imag], axis=1)
    phase_z = (omega * slow[2])[:, None] * z_coord[None, :]
    depth_real = jnp.cos(phase_z).astype(jnp.bfloat16)
    depth_imag = jnp.sin(phase_z).astype(jnp.bfloat16)
    upper_rows = jnp.concatenate([depth_real, -depth_imag], axis=1)
    lower_rows = jnp.concatenate([depth_imag, depth_real], axis=1)
    right_side = jnp.concatenate([upper_rows, lower_rows], axis=0)
    return jnp.dot(left_side, right_side, preferred_element_type=jnp.float32)


def tile_power(lag_row, slow_rows, spectra):
    aligned = align_rows(spectra, lag_row)

    def step(total, freq):
        row = lax.dynamic_index_in_dim(aligned, freq, 0, keepdims=False)
        beams = beam_freq(freq, row, slow_rows)
        squares = beams * beams
        return total + squares[:, :CZ] + squares[:, CZ:], None

    total, unused = lax.scan(step, jnp.zeros((CX * CY, CZ), jnp.float32), jnp.arange(FREQS, dtype=jnp.int32))
    return (total / (FREQS * STATIONS) + BACKGROUND).reshape(CX, CY, CZ)


def to_grid(tiles):
    return tiles.reshape(TY, TX, CX, CY, CZ).transpose(1, 2, 0, 3, 4).reshape(TX * CX, TY * CY, CZ)


def to_tiles(volume):
    return volume.reshape(TX, CX, TY, CY, CZ).transpose(2, 0, 1, 3, 4).reshape(TY * TX, CX, CY, CZ)


def blur(volume, spread_taps):
    for axis in range(3):
        widths = [(0, 0), (0, 0), (0, 0)]
        widths[axis] = (HALF, HALF)
        padded = jnp.pad(volume, widths)
        total = jnp.zeros_like(volume)
        for offset in range(TAPS):
            total = total + spread_taps[axis, offset] * lax.slice_in_dim(padded, offset, offset + volume.shape[axis], axis=axis)
        volume = total
    return volume


def reference(spectra, lag_samples, slowness, spread_taps):
    stacked = lax.map(lambda tile_entry: tile_power(tile_entry[0], tile_entry[1], spectra), (lag_samples, slowness))
    observed = to_grid(stacked)
    estimate = observed
    for sweep in range(ITERS):
        blurred = blur(estimate, spread_taps)
        estimate = estimate * blur(observed / blurred, spread_taps)
    return stacked, to_tiles(estimate)
```

```python
import functools
import math

import jax
import jax.numpy as jnp
from jax import lax
from jax.experimental import pallas as pl
from jax.experimental.pallas import tpu as pltpu
from jax.sharding import PartitionSpec as P

F0 = 600
NT = 6000
TAPS = 17
HALF = 8
ITERS = 4
CX = 32
CY = 8
CZ = 128
LANES = 128

TWO_PI = 2.0 * math.pi
BACKGROUND = 0.05

FA, FB, DA, DB = 0, 16, 32, 64
ENTRIES = 72


def sincos(t):
    u = t * t
    s = t * (1.0 + u * (-1 / 6 + u * (1 / 120 + u * (-1 / 5040 + u * (1 / 362880 - u * (1 / 39916800))))))
    c = 1.0 + u * (-1 / 2 + u * (1 / 24 + u * (-1 / 720 + u * (1 / 40320 - u * (1 / 3628800)))))
    return c, s


def doubled(cs):
    c, s = cs
    t = s + s
    return 1.0 - t * s, t * c


def times(p, q):
    return p[0] * q[0] - p[1] * q[1], p[0] * q[1] + p[1] * q[0]


def beam_kernel(groups, own, width, first_ref, *refs):
    x_refs, (out_ref, xs, com, tab, left, right, acc, work) = refs[:groups], refs[groups:]
    parts = width // LANES
    cols = 2 * width
    for g in range(groups):
        xs[g] = x_refs[g][:, :cols]
        common = x_refs[g][:, cols:].astype(jnp.float32)
        for piece in range(com.shape[1]):
            com[g, piece] = common[:, piece * LANES : (piece + 1) * LANES]
    pieces = com.shape[1]
    bins = (lax.broadcasted_iota(jnp.int32, (own, LANES), 0) + (first_ref[0] + F0)).astype(jnp.float32)
    half_omega = bins * (TWO_PI / NT / 2.0)

    def tables(g, i):
        def common(which):
            index = which * parts + i
            row = com[g, index % pieces, pl.ds(index // pieces, 1), :]
            return jnp.broadcast_to(row, (own, LANES))

        lag = common(0) * 64.0 + common(1)
        turns = bins * lag
        rest = turns - jnp.floor(turns * (1.0 / NT) + 0.5) * float(NT)
        turn = doubled(doubled(sincos(rest * (TWO_PI / NT / 4.0))))
        re = xs[g, :, pl.ds(pl.multiple_of(i * LANES, LANES), LANES)].astype(jnp.float32)
        im = xs[g, :, pl.ds(pl.multiple_of(width + i * LANES, LANES), LANES)].astype(jnp.float32)
        al = re * turn[0] + im * turn[1], im * turn[0] - re * turn[1]

        def put(entry, value):
            tab[i, entry * own : (entry + 1) * own, :] = value

        xl = [sincos(half_omega * common(2))]
        for _ in range(4):
            xl.append(doubled(xl[-1]))
        yl = [sincos(half_omega * common(3))]
        for _ in range(2):
            yl.append(doubled(yl[-1]))

        def products(levels):
            rows = [None]
            for level in levels:
                rows = [level[bit] if row is None else row * level[bit] for bit in range(2) for row in rows]
            return rows

        for entry, value in enumerate(products(yl + xl[:1])):
            put(FA + entry, value)
        for entry, value in enumerate(products(xl[1:])):
            put(FB + entry, value)

        half = sincos(half_omega * common(4))
        rows = [half]
        power = half
        for _ in range(4):
            power = doubled(power)
            rows = rows + [times(row, power) for row in rows]
        for entry, value in enumerate(rows):
            put(DA + entry, value[0])
            put(DA + 16 + entry, value[1])
        e16 = doubled(power)
        e48 = times(e16, doubled(e16))
        for low, high, e in ((0, 3, e48), (1, 2, e16)):
            rc, ms, mc, rs = al[0] * e[0], al[1] * e[1], al[1] * e[0], al[0] * e[1]
            put(DB + high, rc + ms)
            put(DB + 4 + high, mc - rs)
            put(DB + low, rc - ms)
            put(DB + 4 + low, mc + rs)

    def beams(g, f):
        def rows16(entry, i):
            return tab[i, pl.ds(entry * own + f, 16, stride=own), :].astype(jnp.bfloat16)

        def spread(entry, i):
            row = tab[i, pl.ds(entry * own + f, 1), :]
            return jnp.broadcast_to(row, (16, LANES)).astype(jnp.bfloat16)

        for i in range(parts):
            lanes = slice(i * LANES, (i + 1) * LANES)
            a = rows16(FA, i)
            for b in range(16):
                left[b * 16 : (b + 1) * 16, lanes] = a * spread(FB + b, i)
            ar, ai = rows16(DA, i), rows16(DA + 16, i)
            for h in range(4):
                br, bi = spread(DB + h, i), spread(DB + 4 + h, i)
                rr, ii, ri, ir = ar * br, ai * bi, ar * bi, ai * br
                right[h * 32 : h * 32 + 16, lanes] = rr + ii
                right[h * 32 + 16 : h * 32 + 32, lanes] = rr - ii
                right[CZ + h * 32 : CZ + h * 32 + 16, lanes] = ri - ir
                right[CZ + h * 32 + 16 : CZ + h * 32 + 32, lanes] = ri + ir
        got = lax.dot_general(left[...], right[...], (((1,), (1,)), ((), ())), preferred_element_type=jnp.float32)

        @pl.when(g == 0)
        def _():
            acc[f] = got

        @pl.when(g > 0)
        def _():
            acc[f] = acc[f] + got

    def group(g, carry):
        lax.fori_loop(0, parts, lambda i, c: (tables(g, i), c)[1], 0)
        lax.fori_loop(0, own, lambda f, c: (beams(g, f), c)[1], 0)
        return carry

    lax.fori_loop(0, groups, group, 0)

    def butterfly(values, levels):
        for level in range(levels):
            step = 1 << level
            out = list(values)
            for at in range(len(values)):
                if not at & step:
                    (cr, ci), (sr, si) = values[at], values[at + step]
                    out[at] = (cr - si, ci + sr)
                    out[at + step] = (cr + si, ci - sr)
            values = out
        return values

    def power(f, total):
        values = [(acc[f, 8 * x : 8 * x + 8, :CZ], acc[f, 8 * x : 8 * x + 8, CZ:]) for x in range(CX)]
        for x, (re, im) in enumerate(butterfly(values, 5)):
            work[0, 8 * x : 8 * x + 8, :] = re
            work[1, 8 * x : 8 * x + 8, :] = im
        values = [(work[0, pl.ds(y, CX, stride=8), :], work[1, pl.ds(y, CX, stride=8), :]) for y in range(CY)]
        for y, (re, im) in enumerate(butterfly(values, 3)):
            part = re * re + im * im
            prev = out_ref[:, y * CZ : (y + 1) * CZ]
            out_ref[:, y * CZ : (y + 1) * CZ] = jnp.where(f == 0, part, prev + part)
        return total

    lax.fori_loop(0, own, power, 0)
    src = lax.broadcasted_iota(jnp.int32, (CZ, CZ), 0)
    dst = lax.broadcasted_iota(jnp.int32, (CZ, CZ), 1)
    low = src % 16
    place = (src // 32) * 32 + jnp.where((src // 16) % 2 == 0, 16 + low, 15 - low)
    swap = (place == dst).astype(jnp.float32)
    for y in range(CY):
        lanes = slice(y * CZ, (y + 1) * CZ)
        out_ref[:, lanes] = jnp.dot(
            out_ref[:, lanes], swap, precision=lax.Precision.HIGHEST, preferred_element_type=jnp.float32
        )


def split(v):
    high = v.astype(jnp.bfloat16)
    return high, (v - high.astype(jnp.float32)).astype(jnp.bfloat16)


def dot3(a, b):
    dot = functools.partial(jnp.dot, preferred_element_type=jnp.float32)
    return dot(a[0], b[0]) + (dot(a[0], b[1]) + dot(a[1], b[0]))


def deblur_kernel(count, scale, at_ref, taps_ref, own_ref, m2, m1, p1, p2, stacked_ref, est_ref):
    rows, cols = 5 * CX, CY * CZ
    start = (at_ref[0] - 2) * CX

    def inside(first, length):
        x = lax.broadcasted_iota(jnp.int32, (length, cols), 0) + (start + first)
        return (x >= 0) & (x < count * CX)

    stacked = own_ref[...] * scale + BACKGROUND
    halo = [ref[...].astype(jnp.float32) * scale + BACKGROUND for ref in (m2, m1, p1, p2)]
    observed = jnp.concatenate(halo[:2] + [stacked] + halo[2:], axis=0)
    observed = jnp.where(inside(0, rows), observed, 0.0)
    for y in range(CY):
        stacked_ref[:, y, :] = stacked[:, y * CZ : (y + 1) * CZ]

    def band(axis, offset):
        total = jnp.zeros(offset.shape, jnp.float32)
        for tap in range(TAPS):
            total = jnp.where(offset == tap, taps_ref[axis, tap], total)
        return total

    i = lax.broadcasted_iota(jnp.int32, (rows - 2 * HALF, rows), 0)
    p = lax.broadcasted_iota(jnp.int32, (rows - 2 * HALF, rows), 1)
    band_x = split(band(0, p - i))
    w = lax.broadcasted_iota(jnp.int32, (2 * CZ, 2 * CZ), 0)
    k = lax.broadcasted_iota(jnp.int32, (2 * CZ, 2 * CZ), 1)
    band_z = split(band(2, jnp.where(w // CZ == k // CZ, w - k + HALF, -1)))

    def blur(v):
        n = v.shape[0]
        x = dot3(tuple(part[: n - 2 * HALF, :n] for part in band_x), split(v))
        along = []
        for j in range(CY):
            total = None
            for q in range(CY):
                term = taps_ref[1, q - j + HALF] * x[:, q * CZ : (q + 1) * CZ]
                total = term if total is None else total + term
            along.append(total)
        out = []
        for j in range(0, CY, 2):
            out.append(dot3(split(jnp.concatenate(along[j : j + 2], axis=1)), band_z))
        return jnp.concatenate(out, axis=1)

    est, first = observed, 0
    for _ in range(ITERS):
        blurred = blur(est)
        first += HALF
        n = blurred.shape[0]
        ok = inside(first, n)
        ratio = jnp.where(ok, observed[first : first + n] / jnp.where(ok, blurred, 1.0), 0.0)
        change = blur(ratio)
        first += HALF
        est = est[2 * HALF : -2 * HALF] * change
    for y in range(CY):
        est_ref[:, y, :] = est[:, y * CZ : (y + 1) * CZ]


def summed_over(value, axis, size):
    if size & (size - 1):
        return lax.psum(value, axis)
    step = 1
    while step < size:
        value = value + lax.ppermute(value, axis, [(i, i ^ step) for i in range(size)])
        step *= 2
    return value


def per_device(groups, tiles, spectra, lag_samples, slowness, spread_taps):
    freqs, _, width = spectra.shape
    own = freqs // groups
    me = lax.axis_index("sta")
    lag = lag_samples[0]
    common = jnp.concatenate(
        [jnp.stack([lag >> 6, lag & 63]).astype(jnp.bfloat16), slowness[0]], axis=0
    ).reshape(-1)
    room = -(-common.size // (own * LANES)) * own * LANES
    common = jnp.pad(common, (0, room - common.size)).reshape(own, -1)
    flat = spectra.reshape(freqs, 2 * width)

    def bundle(dest):
        return jnp.concatenate([lax.dynamic_slice_in_dim(flat, dest * own, own, 0), common], axis=1)

    blocks = [bundle(me)]
    for k in range(1, groups):
        send = [(i, (i + k) % groups) for i in range(groups)]
        blocks.append(lax.ppermute(bundle((me + k) % groups), "sta", send))

    vmem = pl.BlockSpec(memory_space=pltpu.VMEM)
    smem = pl.BlockSpec(memory_space=pltpu.SMEM)
    pieces = common.shape[1] // LANES
    local = pl.pallas_call(
        functools.partial(beam_kernel, groups, own, width),
        out_shape=jax.ShapeDtypeStruct((CX, CY * CZ), jnp.float32),
        in_specs=[smem] + [vmem] * groups,
        out_specs=vmem,
        scratch_shapes=[
            pltpu.VMEM((groups, own, 2 * width), jnp.bfloat16),
            pltpu.VMEM((groups, pieces, own, LANES), jnp.float32),
            pltpu.VMEM((width // LANES, ENTRIES * own, LANES), jnp.float32),
            pltpu.VMEM((CX * CY, width), jnp.bfloat16),
            pltpu.VMEM((2 * CZ, width), jnp.bfloat16),
            pltpu.VMEM((own, CX * CY, 2 * CZ), jnp.float32),
            pltpu.VMEM((2, CX * CY, CZ), jnp.float32),
        ],
        compiler_params=pltpu.CompilerParams(vmem_limit_bytes=48 * 1024 * 1024),
        name="beams",
    )((me * own).astype(jnp.int32).reshape(1), *blocks)

    total = summed_over(local, "sta", groups)
    narrow = total.astype(jnp.bfloat16)
    halo = []
    for shift in (2, 1, -1, -2):
        moves = [(i, i + shift) for i in range(tiles) if 0 <= i + shift < tiles]
        halo.append(lax.ppermute(narrow, "grid", moves))
    tile = jax.ShapeDtypeStruct((CX, CY, CZ), jnp.float32)
    stacked, deblurred = pl.pallas_call(
        functools.partial(deblur_kernel, tiles, 1.0 / (freqs * width * groups)),
        out_shape=(tile, tile),
        in_specs=[smem, smem] + [vmem] * 5,
        out_specs=(vmem, vmem),
        compiler_params=pltpu.CompilerParams(vmem_limit_bytes=48 * 1024 * 1024),
        name="deblur",
    )(lax.axis_index("grid").astype(jnp.int32).reshape(1), spread_taps, total, *halo)
    return stacked[None], deblurred[None]


def solution(mesh):
    placed = (P(None, None, "sta"), P("grid", "sta"), P("grid", None, "sta"), P())
    return jax.shard_map(
        functools.partial(per_device, mesh.shape["sta"], mesh.shape["grid"]),
        mesh=mesh,
        in_specs=placed,
        out_specs=(P("grid", None, None, None), P("grid", None, None, None)),
        check_vma=False,
    )
```

```python
import functools
import math

import jax
import jax.numpy as jnp
from jax import lax
from jax.experimental import pallas as pl
from jax.experimental.pallas import tpu as pltpu
from jax.sharding import PartitionSpec as P

F0 = 600
NT = 6000
TAPS = 17
HALF = 8
ITERS = 4
CX = 32
CY = 8
CZ = 128
LANES = 128

TWO_PI = 2.0 * math.pi
BACKGROUND = 0.05

FA, FB, DA, DB = 0, 16, 32, 64
ENTRIES = 72


def sincos(t):
    u = t * t
    s = t * (1.0 + u * (-1 / 6 + u * (1 / 120 + u * (-1 / 5040 + u * (1 / 362880 - u * (1 / 39916800))))))
    c = 1.0 + u * (-1 / 2 + u * (1 / 24 + u * (-1 / 720 + u * (1 / 40320 - u * (1 / 3628800)))))
    return c, s


def doubled(cs):
    c, s = cs
    t = s + s
    return 1.0 - t * s, t * c


def times(p, q):
    return p[0] * q[0] - p[1] * q[1], p[0] * q[1] + p[1] * q[0]


def butterfly(values, levels):
    for level in range(levels):
        step = 1 << level
        out = list(values)
        for at in range(len(values)):
            if not at & step:
                (cr, ci), (sr, si) = values[at], values[at + step]
                out[at] = (cr - si, ci + sr)
                out[at + step] = (cr + si, ci - sr)
        values = out
    return values


def beam_kernel(chunks, own, width, first, first_ref, *refs):
    x_refs, refs = refs[:chunks], refs[chunks:]
    if first:
        acc, xs, com, tabs, sides = refs[0], refs[1], refs[2], refs[3:4], refs[4:8]
    else:
        acc_in, out_ref, xs, com, tabs, sides = refs[0], refs[1], refs[2], refs[3], refs[4:6], refs[6:10]
        acc, works, sem = refs[10], refs[11:13], refs[13]
        fetch = pltpu.make_async_copy(acc_in, acc, sem)
        fetch.start()
    parts = width // LANES
    cols = 2 * width
    pieces = com.shape[1]
    for g in range(chunks):
        xs[g] = x_refs[g][:, :cols]
        common = x_refs[g][:, cols:].astype(jnp.float32)
        for piece in range(pieces):
            com[g, piece] = common[:, piece * LANES : (piece + 1) * LANES]
    bins = (lax.broadcasted_iota(jnp.int32, (own, LANES), 0) + (first_ref[0] + F0)).astype(jnp.float32)
    half_omega = bins * (TWO_PI / NT / 2.0)

    def tables(tab, g, i):
        def common(which):
            index = which * parts + i
            row = com[g, index % pieces, pl.ds(index // pieces, 1), :]
            return jnp.broadcast_to(row, (own, LANES))

        lag = common(0) * 64.0 + common(1)
        turns = bins * lag
        rest = turns - jnp.floor(turns * (1.0 / NT) + 0.5) * float(NT)
        turn = doubled(doubled(sincos(rest * (TWO_PI / NT / 4.0))))
        re = xs[g, :, pl.ds(pl.multiple_of(i * LANES, LANES), LANES)].astype(jnp.float32)
        im = xs[g, :, pl.ds(pl.multiple_of(width + i * LANES, LANES), LANES)].astype(jnp.float32)
        al = re * turn[0] + im * turn[1], im * turn[0] - re * turn[1]

        def put(entry, value):
            tab[i, entry * own : (entry + 1) * own, :] = value

        xl = [sincos(half_omega * common(2))]
        for _ in range(4):
            xl.append(doubled(xl[-1]))
        yl = [sincos(half_omega * common(3))]
        for _ in range(2):
            yl.append(doubled(yl[-1]))

        def products(levels):
            rows = [None]
            for level in levels:
                rows = [level[bit] if row is None else row * level[bit] for bit in range(2) for row in rows]
            return rows

        for entry, value in enumerate(products(yl + xl[:1])):
            put(FA + entry, value)
        for entry, value in enumerate(products(xl[1:])):
            put(FB + entry, value)

        half = sincos(half_omega * common(4))
        rows = [half]
        power = half
        for _ in range(4):
            power = doubled(power)
            rows = rows + [times(row, power) for row in rows]
        for entry, value in enumerate(rows):
            put(DA + entry, value[0])
            put(DA + 16 + entry, value[1])
        e16 = doubled(power)
        e48 = times(e16, doubled(e16))
        for low, high, e in ((0, 3, e48), (1, 2, e16)):
            rc, ms, mc, rs = al[0] * e[0], al[1] * e[1], al[1] * e[0], al[0] * e[1]
            put(DB + high, rc + ms)
            put(DB + 4 + high, mc - rs)
            put(DB + low, rc - ms)
            put(DB + 4 + low, mc + rs)

    def operands(tab, side, f):
        left, right = side

        def rows16(entry, i):
            return tab[i, pl.ds(entry * own + f, 16, stride=own), :].astype(jnp.bfloat16)

        def spread(entry, i):
            row = tab[i, pl.ds(entry * own + f, 1), :]
            return jnp.broadcast_to(row, (16, LANES)).astype(jnp.bfloat16)

        for i in range(parts):
            lanes = slice(i * LANES, (i + 1) * LANES)
            a = rows16(FA, i)
            for b in range(16):
                left[b * 16 : (b + 1) * 16, lanes] = a * spread(FB + b, i)
            ar, ai = rows16(DA, i), rows16(DA + 16, i)
            for h in range(4):
                br, bi = spread(DB + h, i), spread(DB + 4 + h, i)
                rr, ii, ri, ir = ar * br, ai * bi, ar * bi, ai * br
                right[h * 32 : h * 32 + 16, lanes] = rr + ii
                right[h * 32 + 16 : h * 32 + 32, lanes] = rr - ii
                right[CZ + h * 32 : CZ + h * 32 + 16, lanes] = ri - ir
                right[CZ + h * 32 + 16 : CZ + h * 32 + 32, lanes] = ri + ir

    def product(side):
        return lax.dot_general(
            side[0][...], side[1][...], (((1,), (1,)), ((), ())), preferred_element_type=jnp.float32
        )

    def add_power(got, work):
        values = [(got[8 * x : 8 * x + 8, :CZ], got[8 * x : 8 * x + 8, CZ:]) for x in range(CX)]
        for x, (re, im) in enumerate(butterfly(values, 5)):
            work[0, 8 * x : 8 * x + 8, :] = re
            work[1, 8 * x : 8 * x + 8, :] = im
        values = [(work[0, pl.ds(y, CX, stride=8), :], work[1, pl.ds(y, CX, stride=8), :]) for y in range(CY)]
        for y, (re, im) in enumerate(butterfly(values, 3)):
            out_ref[:, y * CZ : (y + 1) * CZ] += re * re + im * im

    pairs = (sides[:2], sides[2:])
    batch = 4
    each = parts * batch // own

    def some(n, fn):
        lax.fori_loop(0, n, lambda i, c: (fn(i), c)[1], 0)

    def both(i):
        tables(tabs[0], 0, 2 * i)
        tables(tabs[0], 0, 2 * i + 1)

    some(parts // 2, both)
    if not first:
        out_ref[...] = jnp.zeros_like(out_ref)
        fetch.wait()
    for g in range(chunks):
        last = g == chunks - 1
        tab = tabs[g % len(tabs)]
        operands(tab, pairs[0], 0)

        def block(q, g=g, last=last, tab=tab):
            for j in range(batch):
                f = q * batch + j
                got = product(pairs[j % 2])
                operands(tab, pairs[(j + 1) % 2], jnp.minimum(f + 1, own - 1))
                if first:
                    acc[f] = got
                elif last:
                    add_power(acc[f] + got, works[j % 2])
                else:
                    acc[f] = acc[f] + got
            if not last:
                for e in range(each):
                    tables(tabs[(g + 1) % 2], g + 1, q * each + e)

        some(own // batch, block)

    if first:
        return
    src = lax.broadcasted_iota(jnp.int32, (CZ, CZ), 0)
    dst = lax.broadcasted_iota(jnp.int32, (CZ, CZ), 1)
    low = src % 16
    place = (src // 32) * 32 + jnp.where((src // 16) % 2 == 0, 16 + low, 15 - low)
    swap = (place == dst).astype(jnp.float32)
    for y in range(CY):
        lanes = slice(y * CZ, (y + 1) * CZ)
        out_ref[:, lanes] = jnp.dot(
            out_ref[:, lanes], swap, precision=lax.Precision.HIGHEST, preferred_element_type=jnp.float32
        )


def beams_call(chunks, own, width, pieces, first, *args):
    vmem = pl.BlockSpec(memory_space=pltpu.VMEM)
    smem = pl.BlockSpec(memory_space=pltpu.SMEM)
    rows = CX * CY
    acc = (own, rows, 2 * CZ)
    side = [pltpu.VMEM((rows, width), jnp.bfloat16), pltpu.VMEM((2 * CZ, width), jnp.bfloat16)]
    tab = pltpu.VMEM((width // LANES, ENTRIES * own, LANES), jnp.float32)
    scratch = [
        pltpu.VMEM((chunks, own, 2 * width), jnp.bfloat16),
        pltpu.VMEM((chunks, pieces, own, LANES), jnp.float32),
    ]
    if first:
        scratch += [tab] + side * 2
        out = jax.ShapeDtypeStruct(acc, jnp.float32)
        specs = [smem] + [vmem] * chunks
    else:
        scratch += [tab] * 2 + side * 2 + [pltpu.VMEM(acc, jnp.float32)]
        scratch += [pltpu.VMEM((2, rows, CZ), jnp.float32)] * 2 + [pltpu.SemaphoreType.DMA]
        out = jax.ShapeDtypeStruct((CX, CY * CZ), jnp.float32)
        specs = [smem] + [vmem] * chunks + [pl.BlockSpec(memory_space=pl.ANY)]
    return pl.pallas_call(
        functools.partial(beam_kernel, chunks, own, width, first),
        out_shape=out,
        in_specs=specs,
        out_specs=vmem,
        scratch_shapes=scratch,
        compiler_params=pltpu.CompilerParams(vmem_limit_bytes=48 * 1024 * 1024),
        cost_estimate=pl.CostEstimate(
            flops=2 * chunks * own * rows * 2 * CZ * width, bytes_accessed=8 * own * rows * CZ, transcendentals=0
        ),
        name="beams_own" if first else "beams_rest",
    )(*args)


def split(v):
    high = v.astype(jnp.bfloat16)
    return high, (v - high.astype(jnp.float32)).astype(jnp.bfloat16)


def dot3(a, b):
    dot = functools.partial(jnp.dot, preferred_element_type=jnp.float32)
    return dot(a[0], b[0]) + (dot(a[0], b[1]) + dot(a[1], b[0]))


def deblur_kernel(count, scale, at_ref, taps_ref, own_ref, m2, m1, p1, p2, stacked_ref, est_ref):
    rows, cols = 5 * CX, CY * CZ
    start = (at_ref[0] - 2) * CX

    def inside(first, length):
        x = lax.broadcasted_iota(jnp.int32, (length, cols), 0) + (start + first)
        return (x >= 0) & (x < count * CX)

    stacked = own_ref[...] * scale + BACKGROUND
    halo = [ref[...].astype(jnp.float32) * scale + BACKGROUND for ref in (m2, m1, p1, p2)]
    observed = jnp.concatenate(halo[:2] + [stacked] + halo[2:], axis=0)
    observed = jnp.where(inside(0, rows), observed, 0.0)
    for y in range(CY):
        stacked_ref[:, y, :] = stacked[:, y * CZ : (y + 1) * CZ]

    def band(axis, offset):
        total = jnp.zeros(offset.shape, jnp.float32)
        for tap in range(TAPS):
            total = jnp.where(offset == tap, taps_ref[axis, tap], total)
        return total

    i = lax.broadcasted_iota(jnp.int32, (rows - 2 * HALF, rows), 0)
    p = lax.broadcasted_iota(jnp.int32, (rows - 2 * HALF, rows), 1)
    band_x = split(band(0, p - i))
    w = lax.broadcasted_iota(jnp.int32, (2 * CZ, 2 * CZ), 0)
    k = lax.broadcasted_iota(jnp.int32, (2 * CZ, 2 * CZ), 1)
    band_z = split(band(2, jnp.where(w // CZ == k // CZ, w - k + HALF, -1)))

    def blur(v):
        n = v.shape[0]
        x = dot3(tuple(part[: n - 2 * HALF, :n] for part in band_x), split(v))
        along = []
        for j in range(CY):
            total = None
            for q in range(CY):
                term = taps_ref[1, q - j + HALF] * x[:, q * CZ : (q + 1) * CZ]
                total = term if total is None else total + term
            along.append(total)
        out = []
        for j in range(0, CY, 2):
            out.append(dot3(split(jnp.concatenate(along[j : j + 2], axis=1)), band_z))
        return jnp.concatenate(out, axis=1)

    est, first = observed, 0
    for _ in range(ITERS):
        blurred = blur(est)
        first += HALF
        n = blurred.shape[0]
        ok = inside(first, n)
        ratio = jnp.where(ok, observed[first : first + n] / jnp.where(ok, blurred, 1.0), 0.0)
        change = blur(ratio)
        first += HALF
        est = est[2 * HALF : -2 * HALF] * change
    for y in range(CY):
        est_ref[:, y, :] = est[:, y * CZ : (y + 1) * CZ]


def summed_over(value, axis, size):
    if size & (size - 1):
        return lax.psum(value, axis)
    step = 1
    while step < size:
        value = value + lax.ppermute(value, axis, [(i, i ^ step) for i in range(size)])
        step *= 2
    return value


def per_device(groups, tiles, spectra, lag_samples, slowness, spread_taps):
    freqs, _, width = spectra.shape
    own = freqs // groups
    me = lax.axis_index("sta")
    lag = lag_samples[0]
    common = jnp.concatenate(
        [jnp.stack([lag >> 6, lag & 63]).astype(jnp.bfloat16), slowness[0]], axis=0
    ).reshape(-1)
    room = -(-common.size // (own * LANES)) * own * LANES
    common = jnp.pad(common, (0, room - common.size)).reshape(own, -1)
    flat = spectra.reshape(freqs, 2 * width)

    def bundle(dest):
        return jnp.concatenate([lax.dynamic_slice_in_dim(flat, dest * own, own, 0), common], axis=1)

    blocks = [bundle(me)]
    for k in range(1, groups):
        send = [(i, (i + k) % groups) for i in range(groups)]
        blocks.append(lax.ppermute(bundle((me + k) % groups), "sta", send))

    vmem = pl.BlockSpec(memory_space=pltpu.VMEM)
    smem = pl.BlockSpec(memory_space=pltpu.SMEM)
    pieces = common.shape[1] // LANES
    at = (me * own).astype(jnp.int32).reshape(1)
    held = beams_call(1, own, width, pieces, True, at, blocks[0])
    local = beams_call(groups - 1, own, width, pieces, False, at, *blocks[1:], held)

    total = summed_over(local, "sta", groups)
    narrow = total.astype(jnp.bfloat16)
    halo = []
    for shift in (2, 1, -1, -2):
        moves = [(i, i + shift) for i in range(tiles) if 0 <= i + shift < tiles]
        halo.append(lax.ppermute(narrow, "grid", moves))
    tile = jax.ShapeDtypeStruct((CX, CY, CZ), jnp.float32)
    stacked, deblurred = pl.pallas_call(
        functools.partial(deblur_kernel, tiles, 1.0 / (freqs * width * groups)),
        out_shape=(tile, tile),
        in_specs=[smem, smem] + [vmem] * 5,
        out_specs=(vmem, vmem),
        compiler_params=pltpu.CompilerParams(vmem_limit_bytes=48 * 1024 * 1024),
        name="deblur",
    )(lax.axis_index("grid").astype(jnp.int32).reshape(1), spread_taps, total, *halo)
    return stacked[None], deblurred[None]


def solution(mesh):
    placed = (P(None, None, "sta"), P("grid", "sta"), P("grid", None, "sta"), P())
    return jax.shard_map(
        functools.partial(per_device, mesh.shape["sta"], mesh.shape["grid"]),
        mesh=mesh,
        in_specs=placed,
        out_specs=(P("grid", None, None, None), P("grid", None, None, None)),
        check_vma=False,
    )
```

```python
import functools
import math

import jax
import jax.numpy as jnp
from jax import lax
from jax.experimental import pallas as pl
from jax.experimental.pallas import tpu as pltpu
from jax.sharding import PartitionSpec as P

F0 = 600
NT = 6000
TAPS = 17
HALF = 8
ITERS = 4
CX = 32
CY = 8
CZ = 128
LANES = 128

TWO_PI = 2.0 * math.pi
BACKGROUND = 0.05
SMALLER = 0.25

FA, FB, DA, DB = 0, 16, 32, 64
ENTRIES = 72


def sincos(t):
    u = t * t
    s = t * (1.0 + u * (-1 / 6 + u * (1 / 120 + u * (-1 / 5040 + u * (1 / 362880 - u * (1 / 39916800))))))
    c = 1.0 + u * (-1 / 2 + u * (1 / 24 + u * (-1 / 720 + u * (1 / 40320 - u * (1 / 3628800)))))
    return c, s


def doubled(cs):
    c, s = cs
    t = s + s
    return 1.0 - t * s, t * c


def times(p, q):
    return p[0] * q[0] - p[1] * q[1], p[0] * q[1] + p[1] * q[0]


def butterfly(values, levels):
    for level in range(levels):
        step = 1 << level
        out = list(values)
        for at in range(len(values)):
            if not at & step:
                (cr, ci), (sr, si) = values[at], values[at + step]
                out[at] = (cr - si, ci + sr)
                out[at + step] = (cr + si, ci - sr)
        values = out
    return values


def beam_kernel(chunks, own, width, scale, first_ref, *refs):
    x_refs, refs = refs[:chunks], refs[chunks:]
    first = scale is None
    if first:
        acc, xs, com, tabs = refs[0], refs[1], refs[2], refs[3:4]
    else:
        acc_in, out_ref, xs, com, tabs = refs[0], refs[1], refs[2], refs[3], refs[4:6]
        acc, works, sem = refs[6], refs[7:9], refs[9]
        fetch = pltpu.make_async_copy(acc_in, acc, sem)
        fetch.start()
    parts = width // LANES
    cols = 2 * width
    pieces = com.shape[1]
    for g in range(chunks):
        xs[g] = x_refs[g][:, :cols]
        common = x_refs[g][:, cols:].astype(jnp.float32)
        for piece in range(pieces):
            com[g, piece] = common[:, piece * LANES : (piece + 1) * LANES]
    bins = (lax.broadcasted_iota(jnp.int32, (own, LANES), 0) + (first_ref[0] + F0)).astype(jnp.float32)
    half_omega = bins * (TWO_PI / NT / 2.0)

    def tables(tab, g, i):
        def common(which):
            index = which * parts + i
            row = com[g, index % pieces, pl.ds(index // pieces, 1), :]
            return jnp.broadcast_to(row, (own, LANES))

        lag = common(0) * 64.0 + common(1)
        turns = bins * lag
        rest = turns - jnp.floor(turns * (1.0 / NT) + 0.5) * float(NT)
        turn = doubled(doubled(sincos(rest * (TWO_PI / NT / 4.0))))
        re = xs[g, :, pl.ds(pl.multiple_of(i * LANES, LANES), LANES)].astype(jnp.float32)
        im = xs[g, :, pl.ds(pl.multiple_of(width + i * LANES, LANES), LANES)].astype(jnp.float32)
        al = re * turn[0] + im * turn[1], im * turn[0] - re * turn[1]

        def put(entry, value):
            tab[i, entry * own : (entry + 1) * own, :] = value

        xl = [sincos(half_omega * common(2))]
        for _ in range(4):
            xl.append(doubled(xl[-1]))
        yl = [sincos(half_omega * common(3))]
        for _ in range(2):
            yl.append(doubled(yl[-1]))

        def products(levels):
            rows = [None]
            for level in levels:
                rows = [level[bit] if row is None else row * level[bit] for bit in range(2) for row in rows]
            return rows

        for entry, value in enumerate(products(yl + xl[:1])):
            put(FA + entry, value)
        for entry, value in enumerate(products(xl[1:])):
            put(FB + entry, value)

        half = sincos(half_omega * common(4))
        rows = [half]
        power = half
        for _ in range(4):
            power = doubled(power)
            rows = rows + [times(row, power) for row in rows]
        for entry, value in enumerate(rows):
            put(DA + entry, value[0])
            put(DA + 16 + entry, value[1])
        e16 = doubled(power)
        e48 = times(e16, doubled(e16))
        for low, high, e in ((0, 3, e48), (1, 2, e16)):
            rc, ms, mc, rs = al[0] * e[0], al[1] * e[1], al[1] * e[0], al[0] * e[1]
            put(DB + high, rc + ms)
            put(DB + 4 + high, mc - rs)
            put(DB + low, rc - ms)
            put(DB + 4 + low, mc + rs)

    def beams(tab, f):
        def rows16(entry, i):
            return tab[i, pl.ds(entry * own + f, 16, stride=own), :].astype(jnp.bfloat16)

        def spread(entry, i):
            row = tab[i, pl.ds(entry * own + f, 1), :]
            return jnp.broadcast_to(row, (16, LANES)).astype(jnp.bfloat16)

        left, right = [], []
        for i in range(parts):
            a = rows16(FA, i)
            left.append(jnp.concatenate([a * spread(FB + b, i) for b in range(16)], axis=0))
            ar, ai = rows16(DA, i), rows16(DA + 16, i)
            real, imag = [], []
            for h in range(4):
                br, bi = spread(DB + h, i), spread(DB + 4 + h, i)
                rr, ii, ri, ir = ar * br, ai * bi, ar * bi, ai * br
                real += [rr + ii, rr - ii]
                imag += [ri - ir, ri + ir]
            right.append(jnp.concatenate(real + imag, axis=0))
        return lax.dot_general(
            jnp.concatenate(left, axis=1),
            jnp.concatenate(right, axis=1),
            (((1,), (1,)), ((), ())),
            preferred_element_type=jnp.float32,
        )

    def add_power(got, work):
        values = [(got[8 * x : 8 * x + 8, :CZ], got[8 * x : 8 * x + 8, CZ:]) for x in range(CX)]
        for x, (re, im) in enumerate(butterfly(values, 5)):
            work[0, 8 * x : 8 * x + 8, :] = re
            work[1, 8 * x : 8 * x + 8, :] = im
        values = [(work[0, pl.ds(y, CX, stride=8), :], work[1, pl.ds(y, CX, stride=8), :]) for y in range(CY)]
        for y, (re, im) in enumerate(butterfly(values, 3)):
            out_ref[:, y * CZ : (y + 1) * CZ] += re * re + im * im

    batch = 4
    each = parts * batch // own

    def some(n, fn):
        lax.fori_loop(0, n, lambda i, c: (fn(i), c)[1], 0)

    def both(i):
        tables(tabs[0], 0, 2 * i)
        tables(tabs[0], 0, 2 * i + 1)

    some(parts // 2, both)
    if not first:
        out_ref[...] = jnp.zeros_like(out_ref)
        fetch.wait()
    for g in range(chunks):
        last = g == chunks - 1
        tab = tabs[g % len(tabs)]

        def block(q, g=g, last=last, tab=tab):
            for j in range(batch):
                f = q * batch + j
                got = beams(tab, f)
                if first:
                    acc[f] = got
                elif last:
                    add_power(acc[f] + got, works[j % 2])
                else:
                    acc[f] = acc[f] + got
            if not last:
                for e in range(each):
                    tables(tabs[(g + 1) % 2], g + 1, q * each + e)

        some(own // batch, block)

    if first:
        return
    src = lax.broadcasted_iota(jnp.int32, (CZ, CZ), 0)
    dst = lax.broadcasted_iota(jnp.int32, (CZ, CZ), 1)
    low = src % 16
    place = (src // 32) * 32 + jnp.where((src // 16) % 2 == 0, 16 + low, 15 - low)
    swap = jnp.where(place == dst, scale, 0.0)
    for y in range(CY):
        lanes = slice(y * CZ, (y + 1) * CZ)
        out_ref[:, lanes] = jnp.dot(
            out_ref[:, lanes], swap, precision=lax.Precision.HIGHEST, preferred_element_type=jnp.float32
        )


def beams_call(chunks, own, width, pieces, scale, *args):
    first = scale is None
    vmem = pl.BlockSpec(memory_space=pltpu.VMEM)
    smem = pl.BlockSpec(memory_space=pltpu.SMEM)
    rows = CX * CY
    acc = (own, rows, 2 * CZ)
    tab = pltpu.VMEM((width // LANES, ENTRIES * own, LANES), jnp.float32)
    scratch = [
        pltpu.VMEM((chunks, own, 2 * width), jnp.bfloat16),
        pltpu.VMEM((chunks, pieces, own, LANES), jnp.float32),
    ]
    if first:
        scratch += [tab]
        out = jax.ShapeDtypeStruct(acc, jnp.float32)
        specs = [smem] + [vmem] * chunks
    else:
        scratch += [tab] * 2 + [pltpu.VMEM(acc, jnp.float32)]
        scratch += [pltpu.VMEM((2, rows, CZ), jnp.float32)] * 2 + [pltpu.SemaphoreType.DMA]
        out = jax.ShapeDtypeStruct((CX, CY * CZ), jnp.float32)
        specs = [smem] + [vmem] * chunks + [pl.BlockSpec(memory_space=pl.ANY)]
    return pl.pallas_call(
        functools.partial(beam_kernel, chunks, own, width, scale),
        out_shape=out,
        in_specs=specs,
        out_specs=vmem,
        scratch_shapes=scratch,
        compiler_params=pltpu.CompilerParams(vmem_limit_bytes=48 * 1024 * 1024),
        cost_estimate=pl.CostEstimate(
            flops=2 * chunks * own * rows * 2 * CZ * width, bytes_accessed=8 * own * rows * CZ, transcendentals=0
        ),
        name="beams_own" if first else "beams_rest",
    )(*args)


def split(v):
    high = v.astype(jnp.bfloat16)
    return high, (v - high.astype(jnp.float32)).astype(jnp.bfloat16)


def dot3(a, b):
    dot = functools.partial(jnp.dot, preferred_element_type=jnp.float32)
    return dot(a[0], b[0]) + (dot(a[0], b[1]) + dot(a[1], b[0]))


def deblur_kernel(count, at_ref, taps_ref, own_ref, m2, m1, p1, p2, stacked_ref, est_ref):
    rows, cols = 5 * CX, CY * CZ
    start = (at_ref[0] - 2) * CX

    def inside(first, length):
        x = lax.broadcasted_iota(jnp.int32, (length, cols), 0) + (start + first)
        return (x >= 0) & (x < count * CX)

    stacked = own_ref[...] * (1.0 / SMALLER) + BACKGROUND
    halo = [ref[...].astype(jnp.float32) * (1.0 / SMALLER) + BACKGROUND for ref in (m2, m1, p1, p2)]
    observed = jnp.concatenate(halo[:2] + [stacked] + halo[2:], axis=0)
    observed = jnp.where(inside(0, rows), observed, 0.0)
    for y in range(CY):
        stacked_ref[:, y, :] = stacked[:, y * CZ : (y + 1) * CZ]

    def band(axis, offset):
        total = jnp.zeros(offset.shape, jnp.float32)
        for tap in range(TAPS):
            total = jnp.where(offset == tap, taps_ref[axis, tap], total)
        return total

    i = lax.broadcasted_iota(jnp.int32, (rows - 2 * HALF, rows), 0)
    p = lax.broadcasted_iota(jnp.int32, (rows - 2 * HALF, rows), 1)
    band_x = split(band(0, p - i))
    w = lax.broadcasted_iota(jnp.int32, (2 * CZ, 2 * CZ), 0)
    k = lax.broadcasted_iota(jnp.int32, (2 * CZ, 2 * CZ), 1)
    band_z = split(band(2, jnp.where(w // CZ == k // CZ, w - k + HALF, -1)))

    def blur(v):
        n = v.shape[0]
        x = dot3(tuple(part[: n - 2 * HALF, :n] for part in band_x), split(v))
        along = []
        for j in range(CY):
            total = None
            for q in range(CY):
                term = taps_ref[1, q - j + HALF] * x[:, q * CZ : (q + 1) * CZ]
                total = term if total is None else total + term
            along.append(total)
        out = []
        for j in range(0, CY, 2):
            out.append(dot3(split(jnp.concatenate(along[j : j + 2], axis=1)), band_z))
        return jnp.concatenate(out, axis=1)

    est, first = observed, 0
    for _ in range(ITERS):
        blurred = blur(est)
        first += HALF
        n = blurred.shape[0]
        ok = inside(first, n)
        ratio = jnp.where(ok, observed[first : first + n] / jnp.where(ok, blurred, 1.0), 0.0)
        change = blur(ratio)
        first += HALF
        est = est[2 * HALF : -2 * HALF] * change
    for y in range(CY):
        est_ref[:, y, :] = est[:, y * CZ : (y + 1) * CZ]


def summed_over(value, axis, size):
    if size & (size - 1):
        return lax.psum(value, axis)
    step = 1
    while step < size:
        half = value.astype(jnp.float16)
        other = lax.ppermute(half, axis, [(i, i ^ step) for i in range(size)])
        value = half.astype(jnp.float32) + other.astype(jnp.float32)
        step *= 2
    return value


def per_device(groups, tiles, spectra, lag_samples, slowness, spread_taps):
    freqs, _, width = spectra.shape
    own = freqs // groups
    me = lax.axis_index("sta")
    lag = lag_samples[0]
    common = jnp.concatenate(
        [jnp.stack([lag >> 6, lag & 63]).astype(jnp.bfloat16), slowness[0]], axis=0
    ).reshape(-1)
    room = -(-common.size // (own * LANES)) * own * LANES
    common = jnp.pad(common, (0, room - common.size)).reshape(own, -1)
    flat = spectra.reshape(freqs, 2 * width)

    def bundle(dest):
        return jnp.concatenate([lax.dynamic_slice_in_dim(flat, dest * own, own, 0), common], axis=1)

    blocks = [bundle(me)]
    for k in range(1, groups):
        send = [(i, (i + k) % groups) for i in range(groups)]
        blocks.append(lax.ppermute(bundle((me + k) % groups), "sta", send))

    vmem = pl.BlockSpec(memory_space=pltpu.VMEM)
    smem = pl.BlockSpec(memory_space=pltpu.SMEM)
    pieces = common.shape[1] // LANES
    at = (me * own).astype(jnp.int32).reshape(1)
    scale = SMALLER / (freqs * width * groups)
    held = beams_call(1, own, width, pieces, None, at, blocks[0])
    local = beams_call(groups - 1, own, width, pieces, scale, at, *blocks[1:], held)

    total = summed_over(local, "sta", groups)
    narrow = total.astype(jnp.bfloat16)
    halo = []
    for shift in (2, 1, -1, -2):
        moves = [(i, i + shift) for i in range(tiles) if 0 <= i + shift < tiles]
        halo.append(lax.ppermute(narrow, "grid", moves))
    tile = jax.ShapeDtypeStruct((CX, CY, CZ), jnp.float32)
    stacked, deblurred = pl.pallas_call(
        functools.partial(deblur_kernel, tiles),
        out_shape=(tile, tile),
        in_specs=[smem, smem] + [vmem] * 5,
        out_specs=(vmem, vmem),
        compiler_params=pltpu.CompilerParams(vmem_limit_bytes=48 * 1024 * 1024),
        name="deblur",
    )(lax.axis_index("grid").astype(jnp.int32).reshape(1), spread_taps, total, *halo)
    return stacked[None], deblurred[None]


def solution(mesh):
    placed = (P(None, None, "sta"), P("grid", "sta"), P("grid", None, "sta"), P())
    return jax.shard_map(
        functools.partial(per_device, mesh.shape["sta"], mesh.shape["grid"]),
        mesh=mesh,
        in_specs=placed,
        out_specs=(P("grid", None, None, None), P("grid", None, None, None)),
        check_vma=False,
    )
```

```python
import functools
import math

import jax
import jax.numpy as jnp
from jax import lax
from jax.experimental import pallas as pl
from jax.experimental.pallas import tpu as pltpu
from jax.sharding import PartitionSpec as P

F0 = 600
NT = 6000
TAPS = 17
HALF = 8
ITERS = 4
CX = 32
CY = 8
CZ = 128
LANES = 128

TWO_PI = 2.0 * math.pi
BACKGROUND = 0.05
SMALLER = 0.25

FA, FB, DA, DB = 0, 16, 32, 64
ENTRIES = 72


def sincos(t):
    u = t * t
    s = t * (1.0 + u * (-0.16666600108146667 + u * (0.008329673670232296 - u * 0.00019265798619017005)))
    c = 1.0 + u * (-0.4999999701976776 + u * (0.0416664220392704 + u * (u * 2.4071188818197697e-05 - 0.0013882155762985349)))
    return c, s


def doubled(cs):
    c, s = cs
    t = s + s
    return 1.0 - t * s, t * c


def times(p, q):
    return p[0] * q[0] - p[1] * q[1], p[0] * q[1] + p[1] * q[0]


def butterfly(values, levels):
    for level in range(levels):
        step = 1 << level
        out = list(values)
        for at in range(len(values)):
            if not at & step:
                (cr, ci), (sr, si) = values[at], values[at + step]
                out[at] = (cr - si, ci + sr)
                out[at + step] = (cr + si, ci - sr)
        values = out
    return values


def beam_kernel(chunks, own, width, scale, first_ref, *refs):
    x_refs, refs = refs[:chunks], refs[chunks:]
    first = scale is None
    if first:
        acc, xs, com, tabs = refs[0], refs[1], refs[2], refs[3:4]
    else:
        acc_in, out_ref, xs, com, tabs = refs[0], refs[1], refs[2], refs[3], refs[4:6]
        acc, works, sem = refs[6], refs[7:9], refs[9]
        fetch = pltpu.make_async_copy(acc_in, acc, sem)
        fetch.start()
    parts = width // LANES
    cols = 2 * width
    pieces = com.shape[1]
    for g in range(chunks):
        xs[g] = x_refs[g][:, :cols]
        common = x_refs[g][:, cols:].astype(jnp.float32)
        for piece in range(pieces):
            com[g, piece] = common[:, piece * LANES : (piece + 1) * LANES]
    bins = (lax.broadcasted_iota(jnp.int32, (own, LANES), 0) + (first_ref[0] + F0)).astype(jnp.float32)
    half_omega = bins * (TWO_PI / NT / 2.0)

    def tables(tab, g, i):
        def common(which):
            index = which * parts + i
            row = com[g, index % pieces, pl.ds(index // pieces, 1), :]
            return jnp.broadcast_to(row, (own, LANES))

        lag = common(0) * 64.0 + common(1)
        turns = bins * lag
        rest = turns - jnp.floor(turns * (1.0 / NT) + 0.5) * float(NT)
        turn = doubled(doubled(sincos(rest * (TWO_PI / NT / 4.0))))
        re = xs[g, :, pl.ds(pl.multiple_of(i * LANES, LANES), LANES)].astype(jnp.float32)
        im = xs[g, :, pl.ds(pl.multiple_of(width + i * LANES, LANES), LANES)].astype(jnp.float32)
        al = re * turn[0] + im * turn[1], im * turn[0] - re * turn[1]

        def put(entry, value):
            tab[i, entry * own : (entry + 1) * own, :] = value

        xl = [sincos(half_omega * common(2))]
        for _ in range(4):
            xl.append(doubled(xl[-1]))
        yl = [sincos(half_omega * common(3))]
        for _ in range(2):
            yl.append(doubled(yl[-1]))

        def products(levels):
            rows = [None]
            for level in levels:
                rows = [level[bit] if row is None else row * level[bit] for bit in range(2) for row in rows]
            return rows

        for entry, value in enumerate(products(yl + xl[:1])):
            put(FA + entry, value)
        for entry, value in enumerate(products(xl[1:])):
            put(FB + entry, value)

        half = sincos(half_omega * common(4))
        rows = [half]
        power = half
        for _ in range(4):
            power = doubled(power)
            rows = rows + [times(row, power) for row in rows]
        for entry, value in enumerate(rows):
            put(DA + entry, value[0])
            put(DA + 16 + entry, value[1])
        e16 = doubled(power)
        e48 = times(e16, doubled(e16))
        for low, high, e in ((0, 3, e48), (1, 2, e16)):
            rc, ms, mc, rs = al[0] * e[0], al[1] * e[1], al[1] * e[0], al[0] * e[1]
            put(DB + high, rc + ms)
            put(DB + 4 + high, mc - rs)
            put(DB + low, rc - ms)
            put(DB + 4 + low, mc + rs)

    def beams(tab, f):
        def rows16(entry, i):
            return tab[i, pl.ds(entry * own + f, 16, stride=own), :].astype(jnp.bfloat16)

        def spread(entry, i):
            row = tab[i, pl.ds(entry * own + f, 1), :]
            return jnp.broadcast_to(row, (16, LANES)).astype(jnp.bfloat16)

        left, right = [], []
        for i in range(parts):
            a = rows16(FA, i)
            left.append(jnp.concatenate([a * spread(FB + b, i) for b in range(16)], axis=0))
            ar, ai = rows16(DA, i), rows16(DA + 16, i)
            real, imag = [], []
            for h in range(4):
                br, bi = spread(DB + h, i), spread(DB + 4 + h, i)
                rr, ii, ri, ir = ar * br, ai * bi, ar * bi, ai * br
                real += [rr + ii, rr - ii]
                imag += [ri - ir, ri + ir]
            right.append(jnp.concatenate(real + imag, axis=0))
        return lax.dot_general(
            jnp.concatenate(left, axis=1),
            jnp.concatenate(right, axis=1),
            (((1,), (1,)), ((), ())),
            preferred_element_type=jnp.float32,
        )

    def add_power(got, work):
        values = [(got[8 * x : 8 * x + 8, :CZ], got[8 * x : 8 * x + 8, CZ:]) for x in range(CX)]
        for x, (re, im) in enumerate(butterfly(values, 5)):
            work[0, 8 * x : 8 * x + 8, :] = re
            work[1, 8 * x : 8 * x + 8, :] = im
        values = [(work[0, pl.ds(y, CX, stride=8), :], work[1, pl.ds(y, CX, stride=8), :]) for y in range(CY)]
        for y, (re, im) in enumerate(butterfly(values, 3)):
            out_ref[:, y * CZ : (y + 1) * CZ] += re * re + im * im

    batch = 8
    each = parts * batch // own

    def some(n, fn):
        lax.fori_loop(0, n, lambda i, c: (fn(i), c)[1], 0)

    def both(i):
        tables(tabs[0], 0, 2 * i)
        tables(tabs[0], 0, 2 * i + 1)

    some(parts // 2, both)
    if not first:
        out_ref[...] = jnp.zeros_like(out_ref)
        fetch.wait()
    for g in range(chunks):
        last = g == chunks - 1
        tab = tabs[g % len(tabs)]

        def block(q, g=g, last=last, tab=tab):
            done = 0
            for j in range(batch):
                f = q * batch + j
                got = beams(tab, f)
                if first:
                    acc[f] = got
                elif last:
                    add_power(acc[f] + got, works[j % 2])
                else:
                    acc[f] = acc[f] + got
                while not last and done * batch < (j + 1) * each:
                    tables(tabs[(g + 1) % 2], g + 1, q * each + done)
                    done += 1

        some(own // batch, block)

    if first:
        return
    src = lax.broadcasted_iota(jnp.int32, (CZ, CZ), 0)
    dst = lax.broadcasted_iota(jnp.int32, (CZ, CZ), 1)
    low = src % 16
    place = (src // 32) * 32 + jnp.where((src // 16) % 2 == 0, 16 + low, 15 - low)
    swap = jnp.where(place == dst, scale, 0.0)
    for y in range(CY):
        lanes = slice(y * CZ, (y + 1) * CZ)
        out_ref[:, lanes] = jnp.dot(
            out_ref[:, lanes], swap, precision=lax.Precision.HIGHEST, preferred_element_type=jnp.float32
        )


def beams_call(chunks, own, width, pieces, scale, *args):
    first = scale is None
    vmem = pl.BlockSpec(memory_space=pltpu.VMEM)
    smem = pl.BlockSpec(memory_space=pltpu.SMEM)
    rows = CX * CY
    acc = (own, rows, 2 * CZ)
    tab = pltpu.VMEM((width // LANES, ENTRIES * own, LANES), jnp.float32)
    scratch = [
        pltpu.VMEM((chunks, own, 2 * width), jnp.bfloat16),
        pltpu.VMEM((chunks, pieces, own, LANES), jnp.float32),
    ]
    if first:
        scratch += [tab]
        out = jax.ShapeDtypeStruct(acc, jnp.float32)
        specs = [smem] + [vmem] * chunks
    else:
        scratch += [tab] * 2 + [pltpu.VMEM(acc, jnp.float32)]
        scratch += [pltpu.VMEM((2, rows, CZ), jnp.float32)] * 2 + [pltpu.SemaphoreType.DMA]
        out = jax.ShapeDtypeStruct((CX, CY * CZ), jnp.float32)
        specs = [smem] + [vmem] * chunks + [pl.BlockSpec(memory_space=pl.ANY)]
    return pl.pallas_call(
        functools.partial(beam_kernel, chunks, own, width, scale),
        out_shape=out,
        in_specs=specs,
        out_specs=vmem,
        scratch_shapes=scratch,
        compiler_params=pltpu.CompilerParams(vmem_limit_bytes=48 * 1024 * 1024),
        cost_estimate=pl.CostEstimate(
            flops=2 * chunks * own * rows * 2 * CZ * width, bytes_accessed=8 * own * rows * CZ, transcendentals=0
        ),
        name="beams_own" if first else "beams_rest",
    )(*args)


def split(v):
    high = v.astype(jnp.bfloat16)
    return high, (v - high.astype(jnp.float32)).astype(jnp.bfloat16)


def dot3(a, b):
    dot = functools.partial(jnp.dot, preferred_element_type=jnp.float32)
    return dot(a[0], b[0]) + (dot(a[0], b[1]) + dot(a[1], b[0]))


def deblur_kernel(count, at_ref, taps_ref, own_ref, m2, m1, p1, p2, stacked_ref, est_ref):
    rows, cols = 5 * CX, CY * CZ
    start = (at_ref[0] - 2) * CX

    def inside(first, length):
        x = lax.broadcasted_iota(jnp.int32, (length, cols), 0) + (start + first)
        return (x >= 0) & (x < count * CX)

    stacked = own_ref[...] * (1.0 / SMALLER) + BACKGROUND
    halo = [ref[...].astype(jnp.float32) * (1.0 / SMALLER) + BACKGROUND for ref in (m2, m1, p1, p2)]
    observed = jnp.concatenate(halo[:2] + [stacked] + halo[2:], axis=0)
    observed = jnp.where(inside(0, rows), observed, 0.0)
    for y in range(CY):
        stacked_ref[:, y, :] = stacked[:, y * CZ : (y + 1) * CZ]

    def band(axis, offset):
        total = jnp.zeros(offset.shape, jnp.float32)
        for tap in range(TAPS):
            total = jnp.where(offset == tap, taps_ref[axis, tap], total)
        return total

    i = lax.broadcasted_iota(jnp.int32, (rows - 2 * HALF, rows), 0)
    p = lax.broadcasted_iota(jnp.int32, (rows - 2 * HALF, rows), 1)
    band_x = split(band(0, p - i))
    w = lax.broadcasted_iota(jnp.int32, (2 * CZ, 2 * CZ), 0)
    k = lax.broadcasted_iota(jnp.int32, (2 * CZ, 2 * CZ), 1)
    band_z = split(band(2, jnp.where(w // CZ == k // CZ, w - k + HALF, -1)))

    def blur(v):
        n = v.shape[0]
        x = dot3(tuple(part[: n - 2 * HALF, :n] for part in band_x), split(v))
        along = []
        for j in range(CY):
            total = None
            for q in range(CY):
                term = taps_ref[1, q - j + HALF] * x[:, q * CZ : (q + 1) * CZ]
                total = term if total is None else total + term
            along.append(total)
        out = []
        for j in range(0, CY, 2):
            out.append(dot3(split(jnp.concatenate(along[j : j + 2], axis=1)), band_z))
        return jnp.concatenate(out, axis=1)

    est, first = observed, 0
    for _ in range(ITERS):
        blurred = blur(est)
        first += HALF
        n = blurred.shape[0]
        ok = inside(first, n)
        ratio = jnp.where(ok, observed[first : first + n] / jnp.where(ok, blurred, 1.0), 0.0)
        change = blur(ratio)
        first += HALF
        est = est[2 * HALF : -2 * HALF] * change
    for y in range(CY):
        est_ref[:, y, :] = est[:, y * CZ : (y + 1) * CZ]


def bundle_kernel(groups, own, me_ref, flat_ref, lag_ref, slow_ref, *refs):
    outs, common = refs[:groups], refs[groups]
    cols = flat_ref.shape[1]
    parts = lag_ref.shape[1] // LANES
    pieces = common.shape[1] // LANES
    lag = lag_ref[...]
    slow = slow_ref[...].astype(jnp.float32)
    rows = [(lag >> 6).astype(jnp.float32), (lag & 63).astype(jnp.float32)] + [slow[d : d + 1] for d in range(3)]
    common[...] = jnp.zeros_like(common)
    for index in range(len(rows) * parts):
        row, i = rows[index // parts], index % parts
        at, piece = index // pieces, index % pieces
        common[at : at + 1, piece * LANES : (piece + 1) * LANES] = row[:, i * LANES : (i + 1) * LANES]
    shared = common[...].astype(jnp.bfloat16)
    for k in range(groups):
        dest = me_ref[0] ^ k if groups & (groups - 1) == 0 else lax.rem(me_ref[0] + k, groups)
        outs[k][:, :cols] = flat_ref[pl.ds(pl.multiple_of(dest * own, own), own), :]
        outs[k][:, cols:] = shared


def moves(k, size):
    return [(i, i ^ k if size & (size - 1) == 0 else (i + k) % size) for i in range(size)]


def summed_over(value, axis, size):
    if size & (size - 1):
        return lax.psum(value, axis)
    half = lax.optimization_barrier(value.astype(jnp.float16))
    terms = [half] + [lax.ppermute(half, axis, moves(k, size)) for k in range(1, size)]
    terms = [term.astype(jnp.float32) for term in terms]
    while len(terms) > 1:
        terms = [a + b for a, b in zip(terms[::2], terms[1::2])]
    return terms[0]


def per_device(groups, tiles, spectra, lag_samples, slowness, spread_taps):
    freqs, _, width = spectra.shape
    own = freqs // groups
    me = lax.axis_index("sta").astype(jnp.int32)
    vmem = pl.BlockSpec(memory_space=pltpu.VMEM)
    smem = pl.BlockSpec(memory_space=pltpu.SMEM)
    parts = width // LANES
    pieces = -(-5 * parts // own)
    cols = 2 * width + pieces * LANES
    blocks = pl.pallas_call(
        functools.partial(bundle_kernel, groups, own),
        out_shape=[jax.ShapeDtypeStruct((own, cols), jnp.bfloat16)] * groups,
        in_specs=[smem] + [vmem] * 3,
        out_specs=[vmem] * groups,
        scratch_shapes=[pltpu.VMEM((own, pieces * LANES), jnp.float32)],
        name="bundles",
    )(me.reshape(1), spectra.reshape(freqs, 2 * width), lag_samples, slowness[0])
    blocks = [blocks[0]] + [lax.ppermute(blocks[k], "sta", moves(k, groups)) for k in range(1, groups)]

    at = (me * own).reshape(1)
    scale = SMALLER / (freqs * width * groups)
    held = beams_call(1, own, width, pieces, None, at, blocks[0])
    local = beams_call(groups - 1, own, width, pieces, scale, at, *blocks[1:], held)

    total = summed_over(local, "sta", groups)
    narrow = total.astype(jnp.bfloat16)
    halo = []
    for shift in (2, 1, -1, -2):
        halo.append(lax.ppermute(narrow, "grid", [(i, (i + shift) % tiles) for i in range(tiles)]))
    tile = jax.ShapeDtypeStruct((CX, CY, CZ), jnp.float32)
    stacked, deblurred = pl.pallas_call(
        functools.partial(deblur_kernel, tiles),
        out_shape=(tile, tile),
        in_specs=[smem, smem] + [vmem] * 5,
        out_specs=(vmem, vmem),
        compiler_params=pltpu.CompilerParams(vmem_limit_bytes=48 * 1024 * 1024),
        name="deblur",
    )(lax.axis_index("grid").astype(jnp.int32).reshape(1), spread_taps, total, *halo)
    return stacked[None], deblurred[None]


def solution(mesh):
    placed = (P(None, None, "sta"), P("grid", "sta"), P("grid", None, "sta"), P())
    return jax.shard_map(
        functools.partial(per_device, mesh.shape["sta"], mesh.shape["grid"]),
        mesh=mesh,
        in_specs=placed,
        out_specs=(P("grid", None, None, None), P("grid", None, None, None)),
        check_vma=False,
    )
```

```python
import functools
import math

import jax
import jax.numpy as jnp
from jax import lax
from jax.experimental import pallas as pl
from jax.experimental.pallas import tpu as pltpu
from jax.sharding import PartitionSpec as P

F0 = 600
NT = 6000
TAPS = 17
HALF = 8
ITERS = 4
CX = 32
CY = 8
CZ = 128
LANES = 128

TWO_PI = 2.0 * math.pi
BACKGROUND = 0.05
SMALLER = 0.25

YL, XA, XB, DC, DS, DE, DB = 0, 6, 10, 18, 22, 26, 30
ENTRIES = 38
EXTRA = 3


def sincos(t):
    u = t * t
    s = t * (1.0 + u * (-0.16666600108146667 + u * (0.008329673670232296 - u * 0.00019265798619017005)))
    c = 1.0 + u * (-0.4999999701976776 + u * (0.0416664220392704 + u * (u * 2.4071188818197697e-05 - 0.0013882155762985349)))
    return c, s


def doubled(cs):
    c, s = cs
    t = s + s
    return 1.0 - t * s, t * c


def times(p, q):
    return p[0] * q[0] - p[1] * q[1], p[0] * q[1] + p[1] * q[0]


def butterfly(values, levels):
    for level in range(levels):
        step = 1 << level
        out = list(values)
        for at in range(len(values)):
            if not at & step:
                (cr, ci), (sr, si) = values[at], values[at + step]
                out[at] = (cr - si, ci + sr)
                out[at + step] = (cr + si, ci - sr)
        values = out
    return values


def beam_kernel(chunks, own, width, scale, first_ref, *refs):
    x_refs, refs = refs[:chunks], refs[chunks:]
    first = scale is None
    if first:
        acc, xs, tabs = refs[0], refs[1], refs[2:3]
    else:
        acc_in, out_ref, xs, tabs = refs[0], refs[1], refs[2], refs[3:5]
        acc, works, sem = refs[5], refs[6:8], refs[8]
        fetch = pltpu.make_async_copy(acc_in, acc, sem)
        fetch.start()
    parts = width // LANES
    for g in range(chunks):
        for b in range(own + EXTRA):
            pair = x_refs[g][b].astype(jnp.float32)
            for i in range(parts):
                xs[g, i, 2 * b : 2 * b + 2, :] = pair[:, i * LANES : (i + 1) * LANES]
    bins = (lax.broadcasted_iota(jnp.int32, (own, LANES), 0) + (first_ref[0] + F0)).astype(jnp.float32)
    half_omega = bins * (TWO_PI / NT / 2.0)
    row = lax.broadcasted_iota(jnp.int32, (8, LANES), 0)
    bits = [(row & (1 << level)) != 0 for level in range(3)]
    away = jnp.where(row < 4, 3 - row, row - 4)
    near = (away & 1) != 0, away >= 2
    sign = jnp.where(row < 4, -1.0, 1.0)

    def tables(tab, g, i):
        def common(which):
            at = 2 * own + which
            return jnp.broadcast_to(xs[g, i, at : at + 1, :], (own, LANES))

        lag = common(0) * 64.0 + common(1)
        turns = bins * lag
        rest = turns - jnp.floor(turns * (1.0 / NT) + 0.5) * float(NT)
        turn = doubled(doubled(sincos(rest * (TWO_PI / NT / 4.0))))
        re = xs[g, i, pl.ds(0, own, stride=2), :]
        im = xs[g, i, pl.ds(1, own, stride=2), :]
        al = re * turn[0] + im * turn[1], im * turn[0] - re * turn[1]

        def put(entry, value):
            tab[i, entry * own : (entry + 1) * own, :] = value

        xl = [sincos(half_omega * common(2))]
        for _ in range(4):
            xl.append(doubled(xl[-1]))
        yl = [sincos(half_omega * common(3))]
        for _ in range(2):
            yl.append(doubled(yl[-1]))

        def products(levels):
            rows = [None]
            for level in levels:
                rows = [level[bit] if row is None else row * level[bit] for bit in range(2) for row in rows]
            return rows

        for level in range(3):
            put(YL + 2 * level, yl[level][0])
            put(YL + 2 * level + 1, yl[level][1])
        for entry, value in enumerate(products(xl[:2])):
            put(XA + entry, value)
        for entry, value in enumerate(products(xl[2:])):
            put(XB + entry, value)

        half = sincos(half_omega * common(4))
        e1 = doubled(half)
        e2 = doubled(e1)
        rows = [half, times(half, e1)]
        rows += [times(e, e2) for e in rows]
        for entry, value in enumerate(rows):
            put(DC + entry, value[0])
            put(DS + entry, value[1])
        e4 = doubled(e2)
        e8 = doubled(e4)
        for entry, value in enumerate(e4 + times(e4, e8)):
            put(DE + entry, value)
        e16 = doubled(e8)
        e48 = times(e16, doubled(e16))
        for low, high, e in ((0, 3, e48), (1, 2, e16)):
            rc, ms, mc, rs = al[0] * e[0], al[1] * e[1], al[1] * e[0], al[0] * e[1]
            put(DB + high, rc + ms)
            put(DB + 4 + high, mc - rs)
            put(DB + low, rc - ms)
            put(DB + 4 + low, mc + rs)

    def beams(tab, f):
        def spread(entry, i, rows=8):
            return jnp.broadcast_to(tab[i, pl.ds(entry * own + f, 1), :], (rows, LANES))

        def narrow(entry, i):
            return spread(entry, i, 16).astype(jnp.bfloat16)

        def pack(low, high):
            return jnp.concatenate([low, high], axis=0).astype(jnp.bfloat16)

        left, right = [], []
        for i in range(parts):
            y = None
            for level in range(3):
                level_y = jnp.where(bits[level], spread(YL + 2 * level + 1, i), spread(YL + 2 * level, i))
                y = level_y if y is None else y * level_y
            xy = [y * spread(XA + k, i) for k in range(4)]
            xy = [pack(xy[0], xy[1]), pack(xy[2], xy[3])]
            rows = []
            for b in range(8):
                by = narrow(XB + b, i)
                rows += [xy[0] * by, xy[1] * by]
            left.append(jnp.concatenate(rows, axis=0))

            def middle(entry):
                e = [spread(entry + k, i) for k in range(4)]
                return jnp.where(near[1], jnp.where(near[0], e[3], e[2]), jnp.where(near[0], e[1], e[0]))

            mc, ms = middle(DC), middle(DS) * sign
            turned = []
            for k in range(2):
                c, s = spread(DE + 2 * k, i), spread(DE + 2 * k + 1, i)
                turned.append((c * mc - s * ms, s * mc + c * ms))
            ar, ai = pack(turned[0][0], turned[1][0]), pack(turned[0][1], turned[1][1])
            real, imag = [], []
            for h in range(4):
                br, bi = narrow(DB + h, i), narrow(DB + 4 + h, i)
                rr, ii, ri, ir = ar * br, ai * bi, ar * bi, ai * br
                real += [rr + ii, rr - ii]
                imag += [ri - ir, ri + ir]
            right.append(jnp.concatenate(real + imag, axis=0))
        return lax.dot_general(
            jnp.concatenate(left, axis=1),
            jnp.concatenate(right, axis=1),
            (((1,), (1,)), ((), ())),
            preferred_element_type=jnp.float32,
        )

    def add_power(got, work):
        values = [(got[8 * x : 8 * x + 8, :CZ], got[8 * x : 8 * x + 8, CZ:]) for x in range(CX)]
        for x, (re, im) in enumerate(butterfly(values, 5)):
            work[0, 8 * x : 8 * x + 8, :] = re
            work[1, 8 * x : 8 * x + 8, :] = im
        values = [(work[0, pl.ds(y, CX, stride=8), :], work[1, pl.ds(y, CX, stride=8), :]) for y in range(CY)]
        for y, (re, im) in enumerate(butterfly(values, 3)):
            out_ref[:, y * CZ : (y + 1) * CZ] += re * re + im * im

    batch = 8
    each = parts * batch // own

    def some(n, fn):
        lax.fori_loop(0, n, lambda i, c: (fn(i), c)[1], 0)

    def both(i):
        tables(tabs[0], 0, 2 * i)
        tables(tabs[0], 0, 2 * i + 1)

    some(parts // 2, both)
    if not first:
        out_ref[...] = jnp.zeros_like(out_ref)
        fetch.wait()
    for g in range(chunks):
        last = g == chunks - 1
        tab = tabs[g % len(tabs)]

        def block(q, g=g, last=last, tab=tab):
            done = 0
            for j in range(batch):
                f = q * batch + j
                got = beams(tab, f)
                if first:
                    acc[f] = got
                elif last:
                    add_power(acc[f] + got, works[j % 2])
                else:
                    acc[f] = acc[f] + got
                while not last and done * batch < (j + 1) * each:
                    tables(tabs[(g + 1) % 2], g + 1, q * each + done)
                    done += 1

        some(own // batch, block)

    if first:
        return
    src = lax.broadcasted_iota(jnp.int32, (CZ, CZ), 0)
    dst = lax.broadcasted_iota(jnp.int32, (CZ, CZ), 1)
    low = src % 16
    place = (src // 32) * 32 + jnp.where((src // 16) % 2 == 0, 16 + low, 15 - low)
    swap = jnp.where(place == dst, scale, 0.0)
    for y in range(CY):
        lanes = slice(y * CZ, (y + 1) * CZ)
        out_ref[:, lanes] = jnp.dot(
            out_ref[:, lanes], swap, precision=lax.Precision.HIGHEST, preferred_element_type=jnp.float32
        )


def beams_call(chunks, own, width, scale, *args):
    first = scale is None
    vmem = pl.BlockSpec(memory_space=pltpu.VMEM)
    smem = pl.BlockSpec(memory_space=pltpu.SMEM)
    rows = CX * CY
    acc = (own, rows, 2 * CZ)
    tab = pltpu.VMEM((width // LANES, ENTRIES * own, LANES), jnp.float32)
    scratch = [pltpu.VMEM((chunks, width // LANES, 2 * (own + EXTRA), LANES), jnp.float32)]
    if first:
        scratch += [tab]
        out = jax.ShapeDtypeStruct(acc, jnp.float32)
        specs = [smem] + [vmem] * chunks
    else:
        scratch += [tab] * 2 + [pltpu.VMEM(acc, jnp.float32)]
        scratch += [pltpu.VMEM((2, rows, CZ), jnp.float32)] * 2 + [pltpu.SemaphoreType.DMA]
        out = jax.ShapeDtypeStruct((CX, CY * CZ), jnp.float32)
        specs = [smem] + [vmem] * chunks + [pl.BlockSpec(memory_space=pl.ANY)]
    return pl.pallas_call(
        functools.partial(beam_kernel, chunks, own, width, scale),
        out_shape=out,
        in_specs=specs,
        out_specs=vmem,
        scratch_shapes=scratch,
        compiler_params=pltpu.CompilerParams(vmem_limit_bytes=48 * 1024 * 1024),
        cost_estimate=pl.CostEstimate(
            flops=2 * chunks * own * rows * 2 * CZ * width, bytes_accessed=8 * own * rows * CZ, transcendentals=0
        ),
        name="beams_own" if first else "beams_rest",
    )(*args)


def split(v):
    high = v.astype(jnp.bfloat16)
    return high, (v - high.astype(jnp.float32)).astype(jnp.bfloat16)


def dot3(a, b):
    dot = functools.partial(jnp.dot, preferred_element_type=jnp.float32)
    return dot(a[0], b[0]) + (dot(a[0], b[1]) + dot(a[1], b[0]))


def deblur_kernel(count, at_ref, taps_ref, own_ref, m2, m1, p1, p2, stacked_ref, est_ref):
    rows, cols = 5 * CX, CY * CZ
    start = (at_ref[0] - 2) * CX

    def inside(first, length):
        x = lax.broadcasted_iota(jnp.int32, (length, cols), 0) + (start + first)
        return (x >= 0) & (x < count * CX)

    stacked = own_ref[...] * (1.0 / SMALLER) + BACKGROUND
    halo = [ref[...].astype(jnp.float32) * (1.0 / SMALLER) + BACKGROUND for ref in (m2, m1, p1, p2)]
    observed = jnp.concatenate(halo[:2] + [stacked] + halo[2:], axis=0)
    observed = jnp.where(inside(0, rows), observed, 0.0)
    for y in range(CY):
        stacked_ref[:, y, :] = stacked[:, y * CZ : (y + 1) * CZ]

    def band(axis, offset):
        total = jnp.zeros(offset.shape, jnp.float32)
        for tap in range(TAPS):
            total = jnp.where(offset == tap, taps_ref[axis, tap], total)
        return total

    i = lax.broadcasted_iota(jnp.int32, (rows - 2 * HALF, rows), 0)
    p = lax.broadcasted_iota(jnp.int32, (rows - 2 * HALF, rows), 1)
    band_x = split(band(0, p - i))
    w = lax.broadcasted_iota(jnp.int32, (2 * CZ, 2 * CZ), 0)
    k = lax.broadcasted_iota(jnp.int32, (2 * CZ, 2 * CZ), 1)
    band_z = split(band(2, jnp.where(w // CZ == k // CZ, w - k + HALF, -1)))

    def blur(v):
        n = v.shape[0]
        x = dot3(tuple(part[: n - 2 * HALF, :n] for part in band_x), split(v))
        along = []
        for j in range(CY):
            total = None
            for q in range(CY):
                term = taps_ref[1, q - j + HALF] * x[:, q * CZ : (q + 1) * CZ]
                total = term if total is None else total + term
            along.append(total)
        out = []
        for j in range(0, CY, 2):
            out.append(dot3(split(jnp.concatenate(along[j : j + 2], axis=1)), band_z))
        return jnp.concatenate(out, axis=1)

    est, first = observed, 0
    for _ in range(ITERS):
        blurred = blur(est)
        first += HALF
        n = blurred.shape[0]
        ok = inside(first, n)
        ratio = jnp.where(ok, observed[first : first + n] / jnp.where(ok, blurred, 1.0), 0.0)
        change = blur(ratio)
        first += HALF
        est = est[2 * HALF : -2 * HALF] * change
    for y in range(CY):
        est_ref[:, y, :] = est[:, y * CZ : (y + 1) * CZ]


def bundle_kernel(groups, own, me_ref, spectra_ref, lag_ref, slow_ref, *refs):
    outs, (lag_in, slow_in, sems) = refs[:groups], refs[groups:]
    small = [
        pltpu.make_async_copy(lag_ref, lag_in, sems.at[groups]),
        pltpu.make_async_copy(slow_ref, slow_in, sems.at[groups + 1]),
    ]
    for copy in small:
        copy.start()
    slices = []
    for k in range(groups):
        dest = me_ref[0] ^ k if groups & (groups - 1) == 0 else lax.rem(me_ref[0] + k, groups)
        slices.append(
            pltpu.make_async_copy(spectra_ref.at[pl.ds(dest * own, own)], outs[k].at[pl.ds(0, own)], sems.at[k])
        )
        slices[k].start()
    for copy in small:
        copy.wait()
    lag = lag_in[...]
    slow = slow_in[...].astype(jnp.float32)
    pairs = [
        jnp.concatenate([(lag >> 6).astype(jnp.float32), (lag & 63).astype(jnp.float32)], axis=0),
        slow[:2],
        jnp.concatenate([slow[2:], slow[2:]], axis=0),
    ]
    for k in range(groups):
        for extra, pair in enumerate(pairs):
            outs[k][own + extra] = pair.astype(jnp.bfloat16)
    for copy in slices:
        copy.wait()


def moves(k, size):
    return [(i, i ^ k if size & (size - 1) == 0 else (i + k) % size) for i in range(size)]


def summed_over(value, axis, size):
    if size & (size - 1):
        return lax.psum(value, axis)
    half = lax.optimization_barrier(value.astype(jnp.float16))
    terms = [half] + [lax.ppermute(half, axis, moves(k, size)) for k in range(1, size)]
    terms = [term.astype(jnp.float32) for term in terms]
    while len(terms) > 1:
        terms = [a + b for a, b in zip(terms[::2], terms[1::2])]
    return terms[0]


def per_device(groups, tiles, spectra, lag_samples, slowness, spread_taps):
    freqs, _, width = spectra.shape
    own = freqs // groups
    me = lax.axis_index("sta").astype(jnp.int32)
    vmem = pl.BlockSpec(memory_space=pltpu.VMEM)
    smem = pl.BlockSpec(memory_space=pltpu.SMEM)
    hbm = pl.BlockSpec(memory_space=pl.ANY)
    blocks = pl.pallas_call(
        functools.partial(bundle_kernel, groups, own),
        out_shape=[jax.ShapeDtypeStruct((own + EXTRA, 2, width), jnp.bfloat16)] * groups,
        in_specs=[smem] + [hbm] * 3,
        out_specs=[vmem] * groups,
        scratch_shapes=[
            pltpu.VMEM((1, width), jnp.int32),
            pltpu.VMEM((3, width), jnp.bfloat16),
            pltpu.SemaphoreType.DMA((groups + 2,)),
        ],
        name="bundles",
    )(me.reshape(1), spectra, lag_samples, slowness[0])
    blocks = [blocks[0]] + [lax.ppermute(blocks[k], "sta", moves(k, groups)) for k in range(1, groups)]

    at = (me * own).reshape(1)
    scale = SMALLER / (freqs * width * groups)
    held = beams_call(1, own, width, None, at, blocks[0])
    local = beams_call(groups - 1, own, width, scale, at, *blocks[1:], held)

    total = summed_over(local, "sta", groups)
    narrow = total.astype(jnp.bfloat16)
    halo = []
    for shift in (2, 1, -1, -2):
        halo.append(lax.ppermute(narrow, "grid", [(i, (i + shift) % tiles) for i in range(tiles)]))
    tile = jax.ShapeDtypeStruct((CX, CY, CZ), jnp.float32)
    stacked, deblurred = pl.pallas_call(
        functools.partial(deblur_kernel, tiles),
        out_shape=(tile, tile),
        in_specs=[smem, smem] + [vmem] * 5,
        out_specs=(vmem, vmem),
        compiler_params=pltpu.CompilerParams(vmem_limit_bytes=48 * 1024 * 1024),
        name="deblur",
    )(lax.axis_index("grid").astype(jnp.int32).reshape(1), spread_taps, total, *halo)
    return stacked[None], deblurred[None]


def solution(mesh):
    placed = (P(None, None, "sta"), P("grid", "sta"), P("grid", None, "sta"), P())
    return jax.shard_map(
        functools.partial(per_device, mesh.shape["sta"], mesh.shape["grid"]),
        mesh=mesh,
        in_specs=placed,
        out_specs=(P("grid", None, None, None), P("grid", None, None, None)),
        check_vma=False,
    )
```

```python
import functools
import math

import jax
import jax.numpy as jnp
from jax import lax
from jax.experimental import pallas as pl
from jax.experimental.pallas import tpu as pltpu
from jax.sharding import PartitionSpec as P

F0 = 600
NT = 6000
TAPS = 17
HALF = 8
ITERS = 4
CX = 32
CY = 8
CZ = 128
LANES = 128

TWO_PI = 2.0 * math.pi
BACKGROUND = 0.05
SMALLER = 0.25

YL, XA, XB, DC, DS, DE, DB = 0, 6, 10, 18, 22, 26, 30
ENTRIES = 38
EXTRA = 3


def sincos(t):
    u = t * t
    s = t * (1.0 + u * (-0.16666600108146667 + u * (0.008329673670232296 - u * 0.00019265798619017005)))
    c = 1.0 + u * (-0.4999999701976776 + u * (0.0416664220392704 + u * (u * 2.4071188818197697e-05 - 0.0013882155762985349)))
    return c, s


def doubled(cs):
    c, s = cs
    t = s + s
    return 1.0 - t * s, t * c


def times(p, q):
    return p[0] * q[0] - p[1] * q[1], p[0] * q[1] + p[1] * q[0]


def butterfly(values, levels):
    for level in range(levels):
        step = 1 << level
        out = list(values)
        for at in range(len(values)):
            if not at & step:
                (cr, ci), (sr, si) = values[at], values[at + step]
                out[at] = (cr - si, ci + sr)
                out[at + step] = (cr + si, ci - sr)
        values = out
    return values


def beam_kernel(chunks, own, width, scale, more, first_ref, *refs):
    x_refs, refs = refs[:chunks], refs[chunks:]
    final = scale is not None
    before = refs[0] if more else None
    out_ref, xs, *refs = refs[more:]
    tabs, refs = refs[: min(chunks, 2)], refs[min(chunks, 2) :]
    works, acc = refs[:2], (refs[2:] if final else [out_ref])
    parts = width // LANES
    for g in range(chunks):
        for b in range(own + EXTRA):
            pair = x_refs[g][b].astype(jnp.float32)
            for i in range(parts):
                xs[g, i, 2 * b : 2 * b + 2, :] = pair[:, i * LANES : (i + 1) * LANES]
    bins = (lax.broadcasted_iota(jnp.int32, (own, LANES), 0) + (first_ref[0] + F0)).astype(jnp.float32)
    half_omega = bins * (TWO_PI / NT / 2.0)
    row = lax.broadcasted_iota(jnp.int32, (8, LANES), 0)
    bits = [(row & (1 << level)) != 0 for level in range(3)]
    away = jnp.where(row < 4, 3 - row, row - 4)
    near = (away & 1) != 0, away >= 2
    sign = jnp.where(row < 4, -1.0, 1.0)

    def tables(tab, g, i):
        def common(which):
            at = 2 * own + which
            return jnp.broadcast_to(xs[g, i, at : at + 1, :], (own, LANES))

        lag = common(0) * 64.0 + common(1)
        turns = bins * lag
        rest = turns - jnp.floor(turns * (1.0 / NT) + 0.5) * float(NT)
        turn = doubled(doubled(sincos(rest * (TWO_PI / NT / 4.0))))
        re = xs[g, i, pl.ds(0, own, stride=2), :]
        im = xs[g, i, pl.ds(1, own, stride=2), :]
        al = re * turn[0] + im * turn[1], im * turn[0] - re * turn[1]

        def put(entry, value):
            tab[i, entry * own : (entry + 1) * own, :] = value

        xl = [sincos(half_omega * common(2))]
        for _ in range(4):
            xl.append(doubled(xl[-1]))
        yl = [sincos(half_omega * common(3))]
        for _ in range(2):
            yl.append(doubled(yl[-1]))

        def products(levels):
            rows = [None]
            for level in levels:
                rows = [level[bit] if row is None else row * level[bit] for bit in range(2) for row in rows]
            return rows

        for level in range(3):
            put(YL + 2 * level, yl[level][0])
            put(YL + 2 * level + 1, yl[level][1])
        for entry, value in enumerate(products(xl[:2])):
            put(XA + entry, value)
        for entry, value in enumerate(products(xl[2:])):
            put(XB + entry, value)

        half = sincos(half_omega * common(4))
        e1 = doubled(half)
        e2 = doubled(e1)
        rows = [half, times(half, e1)]
        rows += [times(e, e2) for e in rows]
        for entry, value in enumerate(rows):
            put(DC + entry, value[0])
            put(DS + entry, value[1])
        e4 = doubled(e2)
        e8 = doubled(e4)
        for entry, value in enumerate(e4 + times(e4, e8)):
            put(DE + entry, value)
        e16 = doubled(e8)
        e48 = times(e16, doubled(e16))
        for low, high, e in ((0, 3, e48), (1, 2, e16)):
            rc, ms, mc, rs = al[0] * e[0], al[1] * e[1], al[1] * e[0], al[0] * e[1]
            put(DB + high, rc + ms)
            put(DB + 4 + high, mc - rs)
            put(DB + low, rc - ms)
            put(DB + 4 + low, mc + rs)

    def beams(tab, f):
        def spread(entry, i, rows=8):
            return jnp.broadcast_to(tab[i, pl.ds(entry * own + f, 1), :], (rows, LANES))

        def narrow(entry, i):
            return spread(entry, i, 16).astype(jnp.bfloat16)

        def pack(low, high):
            return jnp.concatenate([low, high], axis=0).astype(jnp.bfloat16)

        left, right = [], []
        for i in range(parts):
            y = None
            for level in range(3):
                level_y = jnp.where(bits[level], spread(YL + 2 * level + 1, i), spread(YL + 2 * level, i))
                y = level_y if y is None else y * level_y
            xy = [y * spread(XA + k, i) for k in range(4)]
            xy = [pack(xy[0], xy[1]), pack(xy[2], xy[3])]
            rows = []
            for b in range(8):
                by = narrow(XB + b, i)
                rows += [xy[0] * by, xy[1] * by]
            left.append(jnp.concatenate(rows, axis=0))

            def middle(entry):
                e = [spread(entry + k, i) for k in range(4)]
                return jnp.where(near[1], jnp.where(near[0], e[3], e[2]), jnp.where(near[0], e[1], e[0]))

            mc, ms = middle(DC), middle(DS) * sign
            turned = []
            for k in range(2):
                c, s = spread(DE + 2 * k, i), spread(DE + 2 * k + 1, i)
                turned.append((c * mc - s * ms, s * mc + c * ms))
            ar, ai = pack(turned[0][0], turned[1][0]), pack(turned[0][1], turned[1][1])
            real, imag = [], []
            for h in range(4):
                br, bi = narrow(DB + h, i), narrow(DB + 4 + h, i)
                rr, ii, ri, ir = ar * br, ai * bi, ar * bi, ai * br
                real += [rr + ii, rr - ii]
                imag += [ri - ir, ri + ir]
            right.append(jnp.concatenate(real + imag, axis=0))
        return lax.dot_general(
            jnp.concatenate(left, axis=1),
            jnp.concatenate(right, axis=1),
            (((1,), (1,)), ((), ())),
            preferred_element_type=jnp.float32,
        )

    def add_power(got, work):
        values = [(got[8 * x : 8 * x + 8, :CZ], got[8 * x : 8 * x + 8, CZ:]) for x in range(CX)]
        for x, (re, im) in enumerate(butterfly(values, 5)):
            work[0, 8 * x : 8 * x + 8, :] = re
            work[1, 8 * x : 8 * x + 8, :] = im
        values = [(work[0, pl.ds(y, CX, stride=8), :], work[1, pl.ds(y, CX, stride=8), :]) for y in range(CY)]
        for y, (re, im) in enumerate(butterfly(values, 3)):
            out_ref[:, y * CZ : (y + 1) * CZ] += re * re + im * im

    batch = 8
    each = parts * batch // own

    def some(n, fn):
        lax.fori_loop(0, n, lambda i, c: (fn(i), c)[1], 0)

    def both(i):
        tables(tabs[0], 0, 2 * i)
        tables(tabs[0], 0, 2 * i + 1)

    some(parts // 2, both)
    if final:
        out_ref[...] = jnp.zeros_like(out_ref)
    for g in range(chunks):
        last = g == chunks - 1
        tab = tabs[g % len(tabs)]

        def block(q, g=g, last=last, tab=tab):
            done = 0
            for j in range(batch):
                f = q * batch + j
                got = beams(tab, f)
                if g > 0:
                    got = acc[0][f] + got
                elif more:
                    got = before[f] + got
                if final and last:
                    add_power(got, works[j % 2])
                else:
                    acc[0][f] = got
                while not last and done * batch < (j + 1) * each:
                    tables(tabs[(g + 1) % 2], g + 1, q * each + done)
                    done += 1

        some(own // batch, block)

    if not final:
        return
    src = lax.broadcasted_iota(jnp.int32, (CZ, CZ), 0)
    dst = lax.broadcasted_iota(jnp.int32, (CZ, CZ), 1)
    low = src % 16
    place = (src // 32) * 32 + jnp.where((src // 16) % 2 == 0, 16 + low, 15 - low)
    swap = jnp.where(place == dst, scale, 0.0)
    for y in range(CY):
        lanes = slice(y * CZ, (y + 1) * CZ)
        out_ref[:, lanes] = jnp.dot(
            out_ref[:, lanes], swap, precision=lax.Precision.HIGHEST, preferred_element_type=jnp.float32
        )


def beams_call(own, width, scale, at, blocks, held):
    vmem = pl.BlockSpec(memory_space=pltpu.VMEM)
    smem = pl.BlockSpec(memory_space=pltpu.SMEM)
    chunks, more, final = len(blocks), int(held is not None), scale is not None
    rows = CX * CY
    acc = (own, rows, 2 * CZ)
    scratch = [pltpu.VMEM((chunks, width // LANES, 2 * (own + EXTRA), LANES), jnp.float32)]
    scratch += [pltpu.VMEM((width // LANES, ENTRIES * own, LANES), jnp.float32)] * min(chunks, 2)
    if final:
        scratch += [pltpu.VMEM((2, rows, CZ), jnp.float32)] * 2
        scratch += [pltpu.VMEM(acc, jnp.float32)] * (chunks > 1)
    return pl.pallas_call(
        functools.partial(beam_kernel, chunks, own, width, scale, more),
        out_shape=jax.ShapeDtypeStruct((CX, CY * CZ) if final else acc, jnp.float32),
        in_specs=[smem] + [vmem] * (chunks + more),
        out_specs=vmem,
        scratch_shapes=scratch,
        compiler_params=pltpu.CompilerParams(vmem_limit_bytes=36 * 1024 * 1024),
        cost_estimate=pl.CostEstimate(
            flops=2 * chunks * own * rows * 2 * CZ * width, bytes_accessed=8 * own * rows * CZ, transcendentals=0
        ),
        name="beams_last" if final else "beams_more" if more else "beams_own",
    )(at, *blocks, *([held] if more else []))


def split(v):
    high = v.astype(jnp.bfloat16)
    return high, (v - high.astype(jnp.float32)).astype(jnp.bfloat16)


def blur_rows():
    reach = 2 * ITERS * HALF
    sizes = [CX + 2 * (reach - HALF * blur) for blur in range(2 * ITERS + 1)]
    return list(zip(sizes[:-1], sizes[1:]))


def band_kernel(taps_ref, *refs):
    def band(axis, offset, low):
        total = jnp.zeros(offset.shape, jnp.float32)
        for tap in range(TAPS):
            total = jnp.where(offset == tap, taps_ref[axis, tap], total)
        high = total.astype(jnp.bfloat16).astype(jnp.float32)
        return jnp.where(low, total - high, high).astype(jnp.bfloat16)

    for (n, m), ref in zip(blur_rows(), refs):
        i = lax.broadcasted_iota(jnp.int32, (m, 3 * n), 0)
        p = lax.broadcasted_iota(jnp.int32, (m, 3 * n), 1)
        low = (p >= n) & (p < 2 * n)
        p = jnp.where(low, p - n, jnp.where(p >= 2 * n, p - 2 * n, p))
        ref[...] = band(0, p - i, low)
    pair = 2 * CZ
    w = lax.broadcasted_iota(jnp.int32, (pair, pair), 0)
    k = lax.broadcasted_iota(jnp.int32, (pair, pair), 1)
    offset = jnp.where(w // CZ == k // CZ, w - k + HALF, -1)
    for part in range(3):
        refs[-1][part * pair : (part + 1) * pair, :] = band(2, offset, part == 1)


def deblur_kernel(count, at_ref, taps_ref, own_ref, m2, m1, p1, p2, *refs):
    bands, (stacked_ref, est_ref) = refs[:-2], refs[-2:]
    rows = 5 * CX
    start = (at_ref[0] - 2) * CX
    x = lax.broadcasted_iota(jnp.int32, (rows, CZ), 0) + start
    inside = jnp.where((x >= 0) & (x < count * CX), 1.0, 0.0)
    outside = jnp.concatenate([1.0 - inside] * CY, axis=1)
    inside = jnp.concatenate([inside] * CY, axis=1)

    stacked = own_ref[...] * (1.0 / SMALLER) + BACKGROUND
    halo = [ref[...].astype(jnp.float32) * (1.0 / SMALLER) + BACKGROUND for ref in (m2, m1, p1, p2)]
    observed = jnp.concatenate(halo[:2] + [stacked] + halo[2:], axis=0) * inside
    for y in range(CY):
        stacked_ref[:, y, :] = stacked[:, y * CZ : (y + 1) * CZ]

    def blur(v, which):
        n = v.shape[0]
        m = n - 2 * HALF
        high, low = split(v)
        x = jnp.dot(
            bands[which][...], jnp.concatenate([high, high, low], axis=0), preferred_element_type=jnp.float32
        )
        along = []
        for j in range(CY):
            total = None
            for q in range(CY):
                term = taps_ref[1, q - j + HALF] * x[:, q * CZ : (q + 1) * CZ]
                total = term if total is None else total + term
            along.append(total)
        pairs = [jnp.concatenate(along[j : j + 2], axis=1) for j in range(0, CY, 2)]
        high, low = split(jnp.concatenate(pairs, axis=0))
        z = jnp.dot(
            jnp.concatenate([high, high, low], axis=1), bands[-1][...], preferred_element_type=jnp.float32
        )
        return jnp.concatenate([z[k * m : (k + 1) * m] for k in range(CY // 2)], axis=1)

    est, first = observed, 0
    for sweep in range(ITERS):
        blurred = blur(est, 2 * sweep)
        first += HALF
        n = blurred.shape[0]
        ratio = observed[first : first + n] / (blurred + outside[first : first + n])
        change = blur(ratio, 2 * sweep + 1)
        first += HALF
        est = est[2 * HALF : -2 * HALF] * change
    for y in range(CY):
        est_ref[:, y, :] = est[:, y * CZ : (y + 1) * CZ]


def bundle_kernel(groups, own, me_ref, spectra_ref, lag_ref, slow_ref, *refs):
    outs, (lag_in, slow_in, sems) = refs[:groups], refs[groups:]
    small = [
        pltpu.make_async_copy(lag_ref, lag_in, sems.at[groups]),
        pltpu.make_async_copy(slow_ref, slow_in, sems.at[groups + 1]),
    ]
    for copy in small:
        copy.start()
    slices = []
    for k in range(groups):
        dest = me_ref[0] ^ k if groups & (groups - 1) == 0 else lax.rem(me_ref[0] + k, groups)
        slices.append(
            pltpu.make_async_copy(spectra_ref.at[pl.ds(dest * own, own)], outs[k].at[pl.ds(0, own)], sems.at[k])
        )
        slices[k].start()
    for copy in small:
        copy.wait()
    lag = lag_in[...]
    slow = slow_in[...].astype(jnp.float32)
    pairs = [
        jnp.concatenate([(lag >> 6).astype(jnp.float32), (lag & 63).astype(jnp.float32)], axis=0),
        slow[:2],
        jnp.concatenate([slow[2:], slow[2:]], axis=0),
    ]
    for k in range(groups):
        for extra, pair in enumerate(pairs):
            outs[k][own + extra] = pair.astype(jnp.bfloat16)
    for copy in slices:
        copy.wait()


def moves(k, size):
    return [(i, i ^ k if size & (size - 1) == 0 else (i + k) % size) for i in range(size)]


def summed_over(half, axis, size):
    if size & (size - 1):
        return lax.psum(half.astype(jnp.float32), axis)
    terms = [half] + [lax.ppermute(half, axis, moves(k, size)) for k in range(1, size)]
    terms = [term.astype(jnp.float32) for term in terms]
    while len(terms) > 1:
        terms = [a + b for a, b in zip(terms[::2], terms[1::2])]
    return terms[0]


def per_device(groups, tiles, spectra, lag_samples, slowness, spread_taps):
    freqs, _, width = spectra.shape
    own = freqs // groups
    me = lax.axis_index("sta").astype(jnp.int32)
    vmem = pl.BlockSpec(memory_space=pltpu.VMEM)
    smem = pl.BlockSpec(memory_space=pltpu.SMEM)
    hbm = pl.BlockSpec(memory_space=pl.ANY)
    blocks = pl.pallas_call(
        functools.partial(bundle_kernel, groups, own),
        out_shape=[jax.ShapeDtypeStruct((own + EXTRA, 2, width), jnp.bfloat16)] * groups,
        in_specs=[smem] + [hbm] * 3,
        out_specs=[vmem] * groups,
        scratch_shapes=[
            pltpu.VMEM((1, width), jnp.int32),
            pltpu.VMEM((3, width), jnp.bfloat16),
            pltpu.SemaphoreType.DMA((groups + 2,)),
        ],
        compiler_params=pltpu.CompilerParams(vmem_limit_bytes=4 * 1024 * 1024),
        name="bundles",
    )(me.reshape(1), spectra, lag_samples, slowness[0])
    blocks = [blocks[0]] + [lax.ppermute(blocks[k], "sta", moves(k, groups)) for k in range(1, groups)]

    at = (me * own).reshape(1)
    scale = SMALLER / (freqs * width * groups)
    held = beams_call(own, width, None, at, blocks[:1], None)
    if groups > 2:
        held = beams_call(own, width, None, at, blocks[1:2], held)
    local = beams_call(own, width, scale, at, blocks[2 if groups > 2 else 1 :], held)

    half, taps = lax.optimization_barrier((local.astype(jnp.float16), spread_taps))
    shapes = [(m, 3 * n) for n, m in blur_rows()] + [(6 * CZ, 2 * CZ)]
    bands = pl.pallas_call(
        band_kernel,
        out_shape=[jax.ShapeDtypeStruct(shape, jnp.bfloat16) for shape in shapes],
        in_specs=[smem],
        out_specs=[vmem] * len(shapes),
        compiler_params=pltpu.CompilerParams(vmem_limit_bytes=8 * 1024 * 1024),
        cost_estimate=pl.CostEstimate(flops=10**7, bytes_accessed=2 * 10**6, transcendentals=0),
        name="bands",
    )(taps)
    total = summed_over(half, "sta", groups)
    narrow = total.astype(jnp.bfloat16)
    halo = []
    for shift in (2, 1, -1, -2):
        halo.append(lax.ppermute(narrow, "grid", [(i, (i + shift) % tiles) for i in range(tiles)]))
    tile = jax.ShapeDtypeStruct((CX, CY, CZ), jnp.float32)
    stacked, deblurred = pl.pallas_call(
        functools.partial(deblur_kernel, tiles),
        out_shape=(tile, tile),
        in_specs=[smem, smem] + [vmem] * (5 + len(bands)),
        out_specs=(vmem, vmem),
        compiler_params=pltpu.CompilerParams(vmem_limit_bytes=36 * 1024 * 1024),
        name="deblur",
    )(lax.axis_index("grid").astype(jnp.int32).reshape(1), spread_taps, total, *halo, *bands)
    return stacked[None], deblurred[None]


def solution(mesh):
    placed = (P(None, None, "sta"), P("grid", "sta"), P("grid", None, "sta"), P())
    return jax.shard_map(
        functools.partial(per_device, mesh.shape["sta"], mesh.shape["grid"]),
        mesh=mesh,
        in_specs=placed,
        out_specs=(P("grid", None, None, None), P("grid", None, None, None)),
        check_vma=False,
    )
```

```python
import functools
import math

import jax
import jax.numpy as jnp
from jax import lax
from jax.experimental import pallas as pl
from jax.experimental.pallas import tpu as pltpu
from jax.sharding import PartitionSpec as P

F0 = 600
NT = 6000
TAPS = 17
HALF = 8
ITERS = 4
CX = 32
CY = 8
CZ = 128
LANES = 128

TWO_PI = 2.0 * math.pi
BACKGROUND = 0.05
SMALLER = 0.25

YL, XA, XB, DC, DS, DE, DB = 0, 6, 10, 18, 22, 26, 30
ENTRIES = 38
EXTRA = 3


def sincos(t):
    u = t * t
    s = t * (1.0 + u * (-0.16666600108146667 + u * (0.008329673670232296 - u * 0.00019265798619017005)))
    c = 1.0 + u * (-0.4999999701976776 + u * (0.0416664220392704 + u * (u * 2.4071188818197697e-05 - 0.0013882155762985349)))
    return c, s


def doubled(cs):
    c, s = cs
    t = s + s
    return 1.0 - t * s, t * c


def times(p, q):
    return p[0] * q[0] - p[1] * q[1], p[0] * q[1] + p[1] * q[0]


def butterfly(values, levels):
    for level in range(levels):
        step = 1 << level
        out = list(values)
        for at in range(len(values)):
            if not at & step:
                (cr, ci), (sr, si) = values[at], values[at + step]
                out[at] = (cr - si, ci + sr)
                out[at + step] = (cr + si, ci - sr)
        values = out
    return values


def beam_kernel(chunks, own, width, scale, more, first_ref, *refs):
    x_refs, refs = refs[:chunks], refs[chunks:]
    final = scale is not None
    before = refs[0] if more else None
    out_ref, xs, *refs = refs[more:]
    tabs, refs = refs[: min(chunks, 2)], refs[min(chunks, 2) :]
    works, acc = refs[:2], (refs[2:] if final else [out_ref])
    parts = width // LANES
    for g in range(chunks):
        for b in range(own + EXTRA):
            pair = x_refs[g][b].astype(jnp.float32)
            for i in range(parts):
                xs[g, i, 2 * b : 2 * b + 2, :] = pair[:, i * LANES : (i + 1) * LANES]
    bins = (lax.broadcasted_iota(jnp.int32, (own, LANES), 0) + (first_ref[0] + F0)).astype(jnp.float32)
    half_omega = bins * (TWO_PI / NT / 2.0)
    row = lax.broadcasted_iota(jnp.int32, (8, LANES), 0)
    bits = [(row & (1 << level)) != 0 for level in range(3)]
    away = jnp.where(row < 4, 3 - row, row - 4)
    near = (away & 1) != 0, away >= 2
    sign = jnp.where(row < 4, -1.0, 1.0)
    lower = lax.broadcasted_iota(jnp.int32, (CX * CY, CZ), 1) < CZ // 2

    def tables(tab, g, i):
        def common(which):
            at = 2 * own + which
            return jnp.broadcast_to(xs[g, i, at : at + 1, :], (own, LANES))

        lag = common(0) * 64.0 + common(1)
        turns = bins * lag
        rest = turns - jnp.floor(turns * (1.0 / NT) + 0.5) * float(NT)
        turn = doubled(doubled(sincos(rest * (TWO_PI / NT / 4.0))))
        re = xs[g, i, pl.ds(0, own, stride=2), :]
        im = xs[g, i, pl.ds(1, own, stride=2), :]
        al = re * turn[0] + im * turn[1], im * turn[0] - re * turn[1]

        def put(entry, value):
            tab[i, entry * own : (entry + 1) * own, :] = value

        xl = [sincos(half_omega * common(2))]
        for _ in range(4):
            xl.append(doubled(xl[-1]))
        yl = [sincos(half_omega * common(3))]
        for _ in range(2):
            yl.append(doubled(yl[-1]))

        def products(levels):
            rows = [None]
            for level in levels:
                rows = [level[bit] if row is None else row * level[bit] for bit in range(2) for row in rows]
            return rows

        for level in range(3):
            put(YL + 2 * level, yl[level][0])
            put(YL + 2 * level + 1, yl[level][1])
        for entry, value in enumerate(products(xl[:2])):
            put(XA + entry, value)
        for entry, value in enumerate(products(xl[2:])):
            put(XB + entry, value)

        half = sincos(half_omega * common(4))
        e1 = doubled(half)
        e2 = doubled(e1)
        rows = [half, times(half, e1)]
        rows += [times(e, e2) for e in rows]
        for entry, value in enumerate(rows):
            put(DC + entry, value[0])
            put(DS + entry, value[1])
        e4 = doubled(e2)
        e8 = doubled(e4)
        for entry, value in enumerate(e4 + times(e4, e8)):
            put(DE + entry, value)
        e16 = doubled(e8)
        e48 = times(e16, doubled(e16))
        for low, high, e in ((0, 3, e48), (1, 2, e16)):
            rc, ms, mc, rs = al[0] * e[0], al[1] * e[1], al[1] * e[0], al[0] * e[1]
            put(DB + high, rc + ms)
            put(DB + 4 + high, mc - rs)
            put(DB + low, rc - ms)
            put(DB + 4 + low, mc + rs)

    def beams(tab, f):
        def spread(entry, i, rows=8):
            return jnp.broadcast_to(tab[i, pl.ds(entry * own + f, 1), :], (rows, LANES))

        def narrow(entry, i):
            return spread(entry, i, 16).astype(jnp.bfloat16)

        def pack(low, high):
            return jnp.concatenate([low, high], axis=0).astype(jnp.bfloat16)

        left, right = [], []
        for i in range(parts):
            y = None
            for level in range(3):
                level_y = jnp.where(bits[level], spread(YL + 2 * level + 1, i), spread(YL + 2 * level, i))
                y = level_y if y is None else y * level_y
            xy = [y * spread(XA + k, i) for k in range(4)]
            xy = [pack(xy[0], xy[1]), pack(xy[2], xy[3])]
            rows = []
            for b in range(8):
                by = narrow(XB + b, i)
                rows += [xy[0] * by, xy[1] * by]
            left.append(jnp.concatenate(rows, axis=0))

            def middle(entry):
                e = [spread(entry + k, i) for k in range(4)]
                return jnp.where(near[1], jnp.where(near[0], e[3], e[2]), jnp.where(near[0], e[1], e[0]))

            mc, ms = middle(DC), middle(DS) * sign
            turned = []
            for k in range(2):
                c, s = spread(DE + 2 * k, i), spread(DE + 2 * k + 1, i)
                turned.append((c * mc - s * ms, s * mc + c * ms))
            ar, ai = pack(turned[0][0], turned[1][0]), pack(turned[0][1], turned[1][1])
            na = -ai
            br = [narrow(DB + h, i) for h in range(4)]
            bi = [narrow(DB + 4 + h, i) for h in range(4)]
            rows = [ar * b for b in br] + [ar * b for b in bi] + [ai * b for b in bi] + [na * b for b in br]
            right.append(jnp.concatenate(rows, axis=0))
        return lax.dot_general(
            jnp.concatenate(left, axis=1),
            jnp.concatenate(right, axis=1),
            (((1,), (1,)), ((), ())),
            preferred_element_type=jnp.float32,
        )

    def add_power(got, work):
        above, below = got[:, :CZ] + got[:, CZ:], got[:, :CZ] - got[:, CZ:]
        reals = jnp.where(lower, above, pltpu.roll(below, CZ // 2, 1))
        imags = jnp.where(lower, pltpu.roll(above, CZ // 2, 1), below)
        values = [(reals[8 * x : 8 * x + 8], imags[8 * x : 8 * x + 8]) for x in range(CX)]
        for x, (re, im) in enumerate(butterfly(values, 5)):
            work[0, 8 * x : 8 * x + 8, :] = re
            work[1, 8 * x : 8 * x + 8, :] = im
        values = [(work[0, pl.ds(y, CX, stride=8), :], work[1, pl.ds(y, CX, stride=8), :]) for y in range(CY)]
        for y, (re, im) in enumerate(butterfly(values, 3)):
            out_ref[:, y * CZ : (y + 1) * CZ] += re * re + im * im

    batch = 8
    each = parts * batch // own

    def some(n, fn):
        lax.fori_loop(0, n, lambda i, c: (fn(i), c)[1], 0)

    def both(i):
        tables(tabs[0], 0, 2 * i)
        tables(tabs[0], 0, 2 * i + 1)

    some(parts // 2, both)
    if final:
        out_ref[...] = jnp.zeros_like(out_ref)
    for g in range(chunks):
        last = g == chunks - 1
        tab = tabs[g % len(tabs)]

        def block(q, g=g, last=last, tab=tab):
            done = 0
            for j in range(batch):
                f = q * batch + j
                got = beams(tab, f)
                if g > 0:
                    got = acc[0][f] + got
                elif more:
                    got = before[f] + got
                if final and last:
                    add_power(got, works[j % 2])
                else:
                    acc[0][f] = got
                while not last and done * batch < (j + 1) * each:
                    tables(tabs[(g + 1) % 2], g + 1, q * each + done)
                    done += 1

        some(own // batch, block)

    if not final:
        return
    src = lax.broadcasted_iota(jnp.int32, (CZ, CZ), 0)
    dst = lax.broadcasted_iota(jnp.int32, (CZ, CZ), 1)
    low = src % 16
    place = (src // 16) % 4 * 32 + jnp.where(src < CZ // 2, 16 + low, 15 - low)
    swap = jnp.where(place == dst, scale, 0.0)
    for y in range(CY):
        lanes = slice(y * CZ, (y + 1) * CZ)
        out_ref[:, lanes] = jnp.dot(
            out_ref[:, lanes], swap, precision=lax.Precision.HIGHEST, preferred_element_type=jnp.float32
        )


def beams_call(own, width, scale, at, blocks, held):
    vmem = pl.BlockSpec(memory_space=pltpu.VMEM)
    smem = pl.BlockSpec(memory_space=pltpu.SMEM)
    chunks, more, final = len(blocks), int(held is not None), scale is not None
    rows = CX * CY
    acc = (own, rows, 2 * CZ)
    scratch = [pltpu.VMEM((chunks, width // LANES, 2 * (own + EXTRA), LANES), jnp.float32)]
    scratch += [pltpu.VMEM((width // LANES, ENTRIES * own, LANES), jnp.float32)] * min(chunks, 2)
    if final:
        scratch += [pltpu.VMEM((2, rows, CZ), jnp.float32)] * 2
        scratch += [pltpu.VMEM(acc, jnp.float32)] * (chunks > 1)
    return pl.pallas_call(
        functools.partial(beam_kernel, chunks, own, width, scale, more),
        out_shape=jax.ShapeDtypeStruct((CX, CY * CZ) if final else acc, jnp.float32),
        in_specs=[smem] + [vmem] * (chunks + more),
        out_specs=vmem,
        scratch_shapes=scratch,
        compiler_params=pltpu.CompilerParams(vmem_limit_bytes=36 * 1024 * 1024),
        cost_estimate=pl.CostEstimate(
            flops=(8 if more else 0) * chunks * own * rows * CZ * width, bytes_accessed=8, transcendentals=0
        ),
        name="beams_last" if final else "beams_more" if more else "beams_own",
    )(at, *blocks, *([held] if more else []))


def split(v):
    high = v.astype(jnp.bfloat16)
    return high, (v - high.astype(jnp.float32)).astype(jnp.bfloat16)


def blur_rows():
    reach = 2 * ITERS * HALF
    sizes = [CX + 2 * (reach - HALF * blur) for blur in range(2 * ITERS + 1)]
    return list(zip(sizes[:-1], sizes[1:]))


def band_kernel(taps_ref, *refs):
    def band(axis, offset, low):
        total = jnp.zeros(offset.shape, jnp.float32)
        for tap in range(TAPS):
            total = jnp.where(offset == tap, taps_ref[axis, tap], total)
        high = total.astype(jnp.bfloat16).astype(jnp.float32)
        return jnp.where(low, total - high, high).astype(jnp.bfloat16)

    for (n, m), ref in zip(blur_rows(), refs):
        i = lax.broadcasted_iota(jnp.int32, (m, 3 * n), 0)
        p = lax.broadcasted_iota(jnp.int32, (m, 3 * n), 1)
        low = (p >= n) & (p < 2 * n)
        p = jnp.where(low, p - n, jnp.where(p >= 2 * n, p - 2 * n, p))
        ref[...] = band(0, p - i, low)
    pair = 2 * CZ
    w = lax.broadcasted_iota(jnp.int32, (pair, pair), 0)
    k = lax.broadcasted_iota(jnp.int32, (pair, pair), 1)
    offset = jnp.where(w // CZ == k // CZ, w - k + HALF, -1)
    for part in range(3):
        refs[-1][part * pair : (part + 1) * pair, :] = band(2, offset, part == 1)


def deblur_kernel(count, at_ref, taps_ref, own_ref, m2, m1, p1, p2, *refs):
    bands, (stacked_ref, est_ref) = refs[:-2], refs[-2:]
    rows = 5 * CX
    start = (at_ref[0] - 2) * CX
    x = lax.broadcasted_iota(jnp.int32, (rows, CZ), 0) + start
    inside = jnp.where((x >= 0) & (x < count * CX), 1.0, 0.0)
    outside = jnp.concatenate([1.0 - inside] * CY, axis=1)
    inside = jnp.concatenate([inside] * CY, axis=1)

    stacked = own_ref[...] * (1.0 / SMALLER) + BACKGROUND
    halo = [ref[...].astype(jnp.float32) * (1.0 / SMALLER) + BACKGROUND for ref in (m2, m1, p1, p2)]
    observed = jnp.concatenate(halo[:2] + [stacked] + halo[2:], axis=0) * inside
    for y in range(CY):
        stacked_ref[:, y, :] = stacked[:, y * CZ : (y + 1) * CZ]

    def blur(v, which):
        n = v.shape[0]
        m = n - 2 * HALF
        high, low = split(v)
        x = jnp.dot(
            bands[which][...], jnp.concatenate([high, high, low], axis=0), preferred_element_type=jnp.float32
        )
        along = []
        for j in range(CY):
            total = None
            for q in range(CY):
                term = taps_ref[1, q - j + HALF] * x[:, q * CZ : (q + 1) * CZ]
                total = term if total is None else total + term
            along.append(total)
        pairs = [jnp.concatenate(along[j : j + 2], axis=1) for j in range(0, CY, 2)]
        high, low = split(jnp.concatenate(pairs, axis=0))
        z = jnp.dot(
            jnp.concatenate([high, high, low], axis=1), bands[-1][...], preferred_element_type=jnp.float32
        )
        return jnp.concatenate([z[k * m : (k + 1) * m] for k in range(CY // 2)], axis=1)

    est, first = observed, 0
    for sweep in range(ITERS):
        blurred = blur(est, 2 * sweep)
        first += HALF
        n = blurred.shape[0]
        ratio = observed[first : first + n] / (blurred + outside[first : first + n])
        change = blur(ratio, 2 * sweep + 1)
        first += HALF
        est = est[2 * HALF : -2 * HALF] * change
    for y in range(CY):
        est_ref[:, y, :] = est[:, y * CZ : (y + 1) * CZ]


def bundle_kernel(groups, own, me_ref, spectra_ref, lag_ref, slow_ref, *refs):
    outs, (lag_in, slow_in, extra, sems) = refs[:groups], refs[groups:]
    small = [
        pltpu.make_async_copy(lag_ref, lag_in, sems.at[groups]),
        pltpu.make_async_copy(slow_ref, slow_in, sems.at[groups + 1]),
    ]
    for copy in small:
        copy.start()
    slices = []
    for k in range(groups):
        dest = me_ref[0] ^ k if groups & (groups - 1) == 0 else lax.rem(me_ref[0] + k, groups)
        slices.append(
            pltpu.make_async_copy(spectra_ref.at[pl.ds(dest * own, own)], outs[k].at[pl.ds(0, own)], sems.at[k])
        )
        slices[k].start()
    for copy in small:
        copy.wait()
    lag = lag_in[...]
    slow = slow_in[...].astype(jnp.float32)
    pairs = [
        jnp.concatenate([(lag >> 6).astype(jnp.float32), (lag & 63).astype(jnp.float32)], axis=0),
        slow[:2],
        jnp.concatenate([slow[2:], slow[2:]], axis=0),
    ]
    for at, pair in enumerate(pairs):
        extra[at] = pair.astype(jnp.bfloat16)
    for k in range(groups):
        slices.append(pltpu.make_async_copy(extra, outs[k].at[pl.ds(own, EXTRA)], sems.at[groups + 2 + k]))
        slices[-1].start()
    for copy in slices:
        copy.wait()


def moves(k, size):
    return [(i, i ^ k if size & (size - 1) == 0 else (i + k) % size) for i in range(size)]


def summed_over(half, axis, size):
    if size & (size - 1):
        return lax.psum(half.astype(jnp.float32), axis)
    terms = [half] + [lax.ppermute(half, axis, moves(k, size)) for k in range(1, size)]
    terms = [term.astype(jnp.float32) for term in terms]
    while len(terms) > 1:
        terms = [a + b for a, b in zip(terms[::2], terms[1::2])]
    return terms[0]


def per_device(groups, tiles, spectra, lag_samples, slowness, spread_taps):
    freqs, _, width = spectra.shape
    own = freqs // groups
    me = lax.axis_index("sta").astype(jnp.int32)
    vmem = pl.BlockSpec(memory_space=pltpu.VMEM)
    smem = pl.BlockSpec(memory_space=pltpu.SMEM)
    hbm = pl.BlockSpec(memory_space=pl.ANY)
    blocks = pl.pallas_call(
        functools.partial(bundle_kernel, groups, own),
        out_shape=[jax.ShapeDtypeStruct((own + EXTRA, 2, width), jnp.bfloat16)] * groups,
        in_specs=[smem] + [hbm] * 3,
        out_specs=[hbm] * groups,
        scratch_shapes=[
            pltpu.VMEM((1, width), jnp.int32),
            pltpu.VMEM((3, width), jnp.bfloat16),
            pltpu.VMEM((EXTRA, 2, width), jnp.bfloat16),
            pltpu.SemaphoreType.DMA((2 * groups + 2,)),
        ],
        compiler_params=pltpu.CompilerParams(vmem_limit_bytes=60 * 1024 * 1024),
        name="bundles",
    )(me.reshape(1), spectra, lag_samples, slowness[0])
    blocks = [blocks[0]] + [lax.ppermute(blocks[k], "sta", moves(k, groups)) for k in range(1, groups)]

    at = (me * own).reshape(1)
    scale = SMALLER / (freqs * width * groups)
    held = beams_call(own, width, None, at, blocks[:1], None)
    if groups > 2:
        held = beams_call(own, width, None, at, blocks[1:2], held)
    local = beams_call(own, width, scale, at, blocks[2 if groups > 2 else 1 :], held)

    half, taps = lax.optimization_barrier((local.astype(jnp.float16), spread_taps))
    shapes = [(m, 3 * n) for n, m in blur_rows()] + [(6 * CZ, 2 * CZ)]
    bands = pl.pallas_call(
        band_kernel,
        out_shape=[jax.ShapeDtypeStruct(shape, jnp.bfloat16) for shape in shapes],
        in_specs=[smem],
        out_specs=[vmem] * len(shapes),
        compiler_params=pltpu.CompilerParams(vmem_limit_bytes=8 * 1024 * 1024),
        cost_estimate=pl.CostEstimate(flops=10**7, bytes_accessed=2 * 10**6, transcendentals=0),
        name="bands",
    )(taps)
    total = summed_over(half, "sta", groups)
    narrow = total.astype(jnp.bfloat16)
    halo = []
    for shift in (2, 1, -1, -2):
        halo.append(lax.ppermute(narrow, "grid", [(i, (i + shift) % tiles) for i in range(tiles)]))
    tile = jax.ShapeDtypeStruct((CX, CY, CZ), jnp.float32)
    stacked, deblurred = pl.pallas_call(
        functools.partial(deblur_kernel, tiles),
        out_shape=(tile, tile),
        in_specs=[smem, smem] + [vmem] * (5 + len(bands)),
        out_specs=(vmem, vmem),
        compiler_params=pltpu.CompilerParams(vmem_limit_bytes=36 * 1024 * 1024),
        name="deblur",
    )(lax.axis_index("grid").astype(jnp.int32).reshape(1), spread_taps, total, *halo, *bands)
    return stacked[None], deblurred[None]


def solution(mesh):
    placed = (P(None, None, "sta"), P("grid", "sta"), P("grid", None, "sta"), P())
    return jax.shard_map(
        functools.partial(per_device, mesh.shape["sta"], mesh.shape["grid"]),
        mesh=mesh,
        in_specs=placed,
        out_specs=(P("grid", None, None, None), P("grid", None, None, None)),
        check_vma=False,
    )
```

```python
import functools
import math

import jax
import jax.numpy as jnp
from jax import lax
from jax.experimental import pallas as pl
from jax.experimental.pallas import tpu as pltpu
from jax.sharding import PartitionSpec as P

F0 = 600
NT = 6000
TAPS = 17
HALF = 8
ITERS = 4
CX = 32
CY = 8
CZ = 128
LANES = 128

TWO_PI = 2.0 * math.pi
BACKGROUND = 0.05
SMALLER = 0.25

YL, XA, XB, DC, DS, DE, DB = 0, 6, 10, 18, 22, 26, 30
ENTRIES = 38
EXTRA = 3


def sincos(t):
    u = t * t
    s = t * (1.0 + u * (-0.16666600108146667 + u * (0.008329673670232296 - u * 0.00019265798619017005)))
    c = 1.0 + u * (-0.4999999701976776 + u * (0.0416664220392704 + u * (u * 2.4071188818197697e-05 - 0.0013882155762985349)))
    return c, s


def doubled(cs):
    c, s = cs
    t = s + s
    return 1.0 - t * s, t * c


def times(p, q):
    return p[0] * q[0] - p[1] * q[1], p[0] * q[1] + p[1] * q[0]


def butterfly(values, levels):
    for level in range(levels):
        step = 1 << level
        out = list(values)
        for at in range(len(values)):
            if not at & step:
                (cr, ci), (sr, si) = values[at], values[at + step]
                out[at] = (cr - si, ci + sr)
                out[at + step] = (cr + si, ci - sr)
        values = out
    return values


def beam_kernel(chunks, own, width, scale, more, first_ref, *refs):
    x_refs, refs = refs[:chunks], refs[chunks:]
    final = scale is not None
    before = refs[0] if more else None
    out_ref, xs, *refs = refs[more:]
    tabs, refs = refs[: min(chunks, 2)], refs[min(chunks, 2) :]
    works, acc = refs[:2], (refs[2:] if final else [out_ref])
    parts = width // LANES
    for g in range(chunks):
        for b in range(own + EXTRA):
            pair = x_refs[g][b].astype(jnp.float32)
            for i in range(parts):
                xs[g, i, 2 * b : 2 * b + 2, :] = pair[:, i * LANES : (i + 1) * LANES]
    bins = (lax.broadcasted_iota(jnp.int32, (own, LANES), 0) + (first_ref[0] + F0)).astype(jnp.float32)
    half_omega = bins * (TWO_PI / NT / 2.0)
    row = lax.broadcasted_iota(jnp.int32, (8, LANES), 0)
    bits = [(row & (1 << level)) != 0 for level in range(3)]
    away = jnp.where(row < 4, 3 - row, row - 4)
    near = (away & 1) != 0, away >= 2
    sign = jnp.where(row < 4, -1.0, 1.0)
    lower = lax.broadcasted_iota(jnp.int32, (CX * CY, CZ), 1) < CZ // 2

    def tables(tab, g, i):
        def common(which):
            at = 2 * own + which
            return jnp.broadcast_to(xs[g, i, at : at + 1, :], (own, LANES))

        lag = common(0) * 64.0 + common(1)
        turns = bins * lag
        rest = turns - jnp.floor(turns * (1.0 / NT) + 0.5) * float(NT)
        turn = doubled(doubled(sincos(rest * (TWO_PI / NT / 4.0))))
        re = xs[g, i, pl.ds(0, own, stride=2), :]
        im = xs[g, i, pl.ds(1, own, stride=2), :]
        al = re * turn[0] + im * turn[1], im * turn[0] - re * turn[1]

        def put(entry, value):
            tab[i, entry * own : (entry + 1) * own, :] = value

        xl = [sincos(half_omega * common(2))]
        for _ in range(4):
            xl.append(doubled(xl[-1]))
        yl = [sincos(half_omega * common(3))]
        for _ in range(2):
            yl.append(doubled(yl[-1]))

        def products(levels):
            rows = [None]
            for level in levels:
                rows = [level[bit] if row is None else row * level[bit] for bit in range(2) for row in rows]
            return rows

        for level in range(3):
            put(YL + 2 * level, yl[level][0])
            put(YL + 2 * level + 1, yl[level][1])
        for entry, value in enumerate(products(xl[:2])):
            put(XA + entry, value)
        for entry, value in enumerate(products(xl[2:])):
            put(XB + entry, value)

        half = sincos(half_omega * common(4))
        e1 = doubled(half)
        e2 = doubled(e1)
        rows = [half, times(half, e1)]
        rows += [times(e, e2) for e in rows]
        for entry, value in enumerate(rows):
            put(DC + entry, value[0])
            put(DS + entry, value[1])
        e4 = doubled(e2)
        e8 = doubled(e4)
        for entry, value in enumerate(e4 + times(e4, e8)):
            put(DE + entry, value)
        e16 = doubled(e8)
        e48 = times(e16, doubled(e16))
        for low, high, e in ((0, 3, e48), (1, 2, e16)):
            rc, ms, mc, rs = al[0] * e[0], al[1] * e[1], al[1] * e[0], al[0] * e[1]
            put(DB + high, rc + ms)
            put(DB + 4 + high, mc - rs)
            put(DB + low, rc - ms)
            put(DB + 4 + low, mc + rs)

    def beams(tab, f):
        def spread(entry, i, rows=8):
            return jnp.broadcast_to(tab[i, pl.ds(entry * own + f, 1), :], (rows, LANES))

        def narrow(entry, i):
            return spread(entry, i, 16).astype(jnp.bfloat16)

        def pack(low, high):
            return jnp.concatenate([low, high], axis=0).astype(jnp.bfloat16)

        left, right = [], []
        for i in range(parts):
            y = None
            for level in range(3):
                level_y = jnp.where(bits[level], spread(YL + 2 * level + 1, i), spread(YL + 2 * level, i))
                y = level_y if y is None else y * level_y
            xy = [y * spread(XA + k, i) for k in range(4)]
            xy = [pack(xy[0], xy[1]), pack(xy[2], xy[3])]
            rows = []
            for b in range(8):
                by = narrow(XB + b, i)
                rows += [xy[0] * by, xy[1] * by]
            left.append(jnp.concatenate(rows, axis=0))

            def middle(entry):
                e = [spread(entry + k, i) for k in range(4)]
                return jnp.where(near[1], jnp.where(near[0], e[3], e[2]), jnp.where(near[0], e[1], e[0]))

            mc, ms = middle(DC), middle(DS) * sign
            turned = []
            for k in range(2):
                c, s = spread(DE + 2 * k, i), spread(DE + 2 * k + 1, i)
                turned.append((c * mc - s * ms, s * mc + c * ms))
            ar, ai = pack(turned[0][0], turned[1][0]), pack(turned[0][1], turned[1][1])
            na = -ai
            br = [narrow(DB + h, i) for h in range(4)]
            bi = [narrow(DB + 4 + h, i) for h in range(4)]
            rows = [ar * b for b in br] + [ar * b for b in bi] + [ai * b for b in bi] + [na * b for b in br]
            right.append(jnp.concatenate(rows, axis=0))
        return lax.dot_general(
            jnp.concatenate(left, axis=1),
            jnp.concatenate(right, axis=1),
            (((1,), (1,)), ((), ())),
            preferred_element_type=jnp.float32,
        )

    def add_power(got, work):
        above, below = got[:, :CZ] + got[:, CZ:], got[:, :CZ] - got[:, CZ:]
        reals = jnp.where(lower, above, pltpu.roll(below, CZ // 2, 1))
        imags = jnp.where(lower, pltpu.roll(above, CZ // 2, 1), below)
        values = [(reals[8 * x : 8 * x + 8], imags[8 * x : 8 * x + 8]) for x in range(CX)]
        for x, (re, im) in enumerate(butterfly(values, 5)):
            work[0, 8 * x : 8 * x + 8, :] = re
            work[1, 8 * x : 8 * x + 8, :] = im
        values = [(work[0, pl.ds(y, CX, stride=8), :], work[1, pl.ds(y, CX, stride=8), :]) for y in range(CY)]
        for y, (re, im) in enumerate(butterfly(values, 3)):
            out_ref[:, y * CZ : (y + 1) * CZ] += re * re + im * im

    batch = 8 if final else own
    each = parts * batch // own

    def some(n, fn):
        lax.fori_loop(0, n, lambda i, c: (fn(i), c)[1], 0)

    def both(i):
        tables(tabs[0], 0, 2 * i)
        tables(tabs[0], 0, 2 * i + 1)

    some(parts // 2, both)
    if final:
        out_ref[...] = jnp.zeros_like(out_ref)
    for g in range(chunks):
        last = g == chunks - 1
        tab = tabs[g % len(tabs)]

        def block(q, g=g, last=last, tab=tab):
            done = 0
            for j in range(batch):
                f = q * batch + j
                got = beams(tab, f)
                if g > 0:
                    got = acc[0][f] + got
                elif more:
                    got = before[f] + got
                if final and last:
                    add_power(got, works[j % 2])
                else:
                    acc[0][f] = got
                while not last and done * batch < (j + 1) * each:
                    tables(tabs[(g + 1) % 2], g + 1, q * each + done)
                    done += 1

        some(own // batch, block)

    if not final:
        return
    src = lax.broadcasted_iota(jnp.int32, (CZ, CZ), 0)
    dst = lax.broadcasted_iota(jnp.int32, (CZ, CZ), 1)
    low = src % 16
    place = (src // 16) % 4 * 32 + jnp.where(src < CZ // 2, 16 + low, 15 - low)
    swap = jnp.where(place == dst, scale, 0.0)
    blocks = [out_ref[:, y * CZ : (y + 1) * CZ] for y in range(CY)]
    natural = jnp.dot(
        jnp.concatenate(blocks, axis=0), swap, precision=lax.Precision.HIGHEST, preferred_element_type=jnp.float32
    )
    for y in range(CY):
        out_ref[:, y * CZ : (y + 1) * CZ] = natural[y * CX : (y + 1) * CX]


def beams_call(own, width, scale, at, blocks, held):
    vmem = pl.BlockSpec(memory_space=pltpu.VMEM)
    smem = pl.BlockSpec(memory_space=pltpu.SMEM)
    chunks, more, final = len(blocks), int(held is not None), scale is not None
    rows = CX * CY
    acc = (own, rows, 2 * CZ)
    scratch = [pltpu.VMEM((chunks, width // LANES, 2 * (own + EXTRA), LANES), jnp.float32)]
    scratch += [pltpu.VMEM((width // LANES, ENTRIES * own, LANES), jnp.float32)] * min(chunks, 2)
    if final:
        scratch += [pltpu.VMEM((2, rows, CZ), jnp.float32)] * 2
        scratch += [pltpu.VMEM(acc, jnp.float32)] * (chunks > 1)
    return pl.pallas_call(
        functools.partial(beam_kernel, chunks, own, width, scale, more),
        out_shape=jax.ShapeDtypeStruct((CX, CY * CZ) if final else acc, jnp.float32),
        in_specs=[smem] + [vmem] * (chunks + more),
        out_specs=vmem,
        scratch_shapes=scratch,
        compiler_params=pltpu.CompilerParams(vmem_limit_bytes=36 * 1024 * 1024),
        cost_estimate=pl.CostEstimate(
            flops=(8 if more else 0) * chunks * own * rows * CZ * width, bytes_accessed=8, transcendentals=0
        ),
        name="beams_last" if final else "beams_more" if more else "beams_own",
    )(at, *blocks, *([held] if more else []))


def split(v):
    high = v.astype(jnp.bfloat16)
    return high, (v - high.astype(jnp.float32)).astype(jnp.bfloat16)


def blur_rows():
    reach = 2 * ITERS * HALF
    sizes = [CX + 2 * (reach - HALF * blur) for blur in range(2 * ITERS + 1)]
    return list(zip(sizes[:-1], sizes[1:]))


def band_kernel(taps_ref, *refs):
    def band(axis, offset, low):
        total = jnp.zeros(offset.shape, jnp.float32)
        for tap in range(TAPS):
            total = jnp.where(offset == tap, taps_ref[axis, tap], total)
        high = total.astype(jnp.bfloat16).astype(jnp.float32)
        return jnp.where(low, total - high, high).astype(jnp.bfloat16)

    for (n, m), ref in zip(blur_rows(), refs):
        i = lax.broadcasted_iota(jnp.int32, (m, 3 * n), 0)
        p = lax.broadcasted_iota(jnp.int32, (m, 3 * n), 1)
        low = (p >= n) & (p < 2 * n)
        p = jnp.where(low, p - n, jnp.where(p >= 2 * n, p - 2 * n, p))
        ref[...] = band(0, p - i, low)
    pair = 2 * CZ
    w = lax.broadcasted_iota(jnp.int32, (pair, pair), 0)
    k = lax.broadcasted_iota(jnp.int32, (pair, pair), 1)
    offset = jnp.where(w // CZ == k // CZ, w - k + HALF, -1)
    for part in range(3):
        refs[-1][part * pair : (part + 1) * pair, :] = band(2, offset, part == 1)


def deblur_kernel(count, at_ref, taps_ref, own_ref, m2, m1, p1, p2, *refs):
    bands, (stacked_ref, est_ref) = refs[:-2], refs[-2:]
    rows = 5 * CX
    start = (at_ref[0] - 2) * CX
    x = lax.broadcasted_iota(jnp.int32, (rows, CZ), 0) + start
    inside = jnp.where((x >= 0) & (x < count * CX), 1.0, 0.0)
    outside = jnp.concatenate([1.0 - inside] * CY, axis=1)
    inside = jnp.concatenate([inside] * CY, axis=1)

    stacked = own_ref[...] * (1.0 / SMALLER) + BACKGROUND
    halo = [ref[...].astype(jnp.float32) * (1.0 / SMALLER) + BACKGROUND for ref in (m2, m1, p1, p2)]
    observed = jnp.concatenate(halo[:2] + [stacked] + halo[2:], axis=0) * inside
    for y in range(CY):
        stacked_ref[:, y, :] = stacked[:, y * CZ : (y + 1) * CZ]

    def blur(v, which):
        n = v.shape[0]
        m = n - 2 * HALF
        high, low = split(v)
        x = jnp.dot(
            bands[which][...], jnp.concatenate([high, high, low], axis=0), preferred_element_type=jnp.float32
        )
        along = []
        for j in range(CY):
            total = None
            for q in range(CY):
                term = taps_ref[1, q - j + HALF] * x[:, q * CZ : (q + 1) * CZ]
                total = term if total is None else total + term
            along.append(total)
        pairs = [jnp.concatenate(along[j : j + 2], axis=1) for j in range(0, CY, 2)]
        high, low = split(jnp.concatenate(pairs, axis=0))
        z = jnp.dot(
            jnp.concatenate([high, high, low], axis=1), bands[-1][...], preferred_element_type=jnp.float32
        )
        return jnp.concatenate([z[k * m : (k + 1) * m] for k in range(CY // 2)], axis=1)

    est, first = observed, 0
    for sweep in range(ITERS):
        blurred = blur(est, 2 * sweep)
        first += HALF
        n = blurred.shape[0]
        ratio = observed[first : first + n] / (blurred + outside[first : first + n])
        change = blur(ratio, 2 * sweep + 1)
        first += HALF
        est = est[2 * HALF : -2 * HALF] * change
    for y in range(CY):
        est_ref[:, y, :] = est[:, y * CZ : (y + 1) * CZ]


def bundle_kernel(groups, own, me_ref, spectra_ref, lag_ref, slow_ref, *refs):
    outs, (lag_in, slow_in, sems) = refs[:groups], refs[groups:]
    small = [
        pltpu.make_async_copy(lag_ref, lag_in, sems.at[groups]),
        pltpu.make_async_copy(slow_ref, slow_in, sems.at[groups + 1]),
    ]
    for copy in small:
        copy.start()
    slices = []
    for k in range(groups):
        dest = me_ref[0] ^ k if groups & (groups - 1) == 0 else lax.rem(me_ref[0] + k, groups)
        slices.append(
            pltpu.make_async_copy(spectra_ref.at[pl.ds(dest * own, own)], outs[k].at[pl.ds(0, own)], sems.at[k])
        )
        slices[k].start()
    for copy in small:
        copy.wait()
    lag = lag_in[...]
    slow = slow_in[...].astype(jnp.float32)
    pairs = [
        jnp.concatenate([(lag >> 6).astype(jnp.float32), (lag & 63).astype(jnp.float32)], axis=0),
        slow[:2],
        jnp.concatenate([slow[2:], slow[2:]], axis=0),
    ]
    for k in range(groups):
        for extra, pair in enumerate(pairs):
            outs[k][own + extra] = pair.astype(jnp.bfloat16)
    for copy in slices:
        copy.wait()


def moves(k, size):
    return [(i, i ^ k if size & (size - 1) == 0 else (i + k) % size) for i in range(size)]


def summed_over(half, axis, size):
    if size & (size - 1):
        return lax.psum(half.astype(jnp.float32), axis)
    terms = [half] + [lax.ppermute(half, axis, moves(k, size)) for k in range(1, size)]
    terms = [term.astype(jnp.float32) for term in terms]
    while len(terms) > 1:
        terms = [a + b for a, b in zip(terms[::2], terms[1::2])]
    return terms[0]


def per_device(groups, tiles, spectra, lag_samples, slowness, spread_taps):
    freqs, _, width = spectra.shape
    own = freqs // groups
    me = lax.axis_index("sta").astype(jnp.int32)
    vmem = pl.BlockSpec(memory_space=pltpu.VMEM)
    smem = pl.BlockSpec(memory_space=pltpu.SMEM)
    hbm = pl.BlockSpec(memory_space=pl.ANY)
    blocks = pl.pallas_call(
        functools.partial(bundle_kernel, groups, own),
        out_shape=[jax.ShapeDtypeStruct((own + EXTRA, 2, width), jnp.bfloat16)] * groups,
        in_specs=[smem] + [hbm] * 3,
        out_specs=[vmem] * groups,
        scratch_shapes=[
            pltpu.VMEM((1, width), jnp.int32),
            pltpu.VMEM((3, width), jnp.bfloat16),
            pltpu.SemaphoreType.DMA((groups + 2,)),
        ],
        compiler_params=pltpu.CompilerParams(vmem_limit_bytes=60 * 1024 * 1024),
        name="bundles",
    )(me.reshape(1), spectra, lag_samples, slowness[0])
    blocks = [blocks[0]] + [lax.ppermute(blocks[k], "sta", moves(k, groups)) for k in range(1, groups)]

    at = (me * own).reshape(1)
    scale = SMALLER / (freqs * width * groups)
    held = beams_call(own, width, None, at, blocks[:1], None)
    if groups > 2:
        held = beams_call(own, width, None, at, blocks[1:2], held)
    local = beams_call(own, width, scale, at, blocks[2 if groups > 2 else 1 :], held)

    half, taps = lax.optimization_barrier((local.astype(jnp.float16), spread_taps))
    shapes = [(m, 3 * n) for n, m in blur_rows()] + [(6 * CZ, 2 * CZ)]
    bands = pl.pallas_call(
        band_kernel,
        out_shape=[jax.ShapeDtypeStruct(shape, jnp.bfloat16) for shape in shapes],
        in_specs=[smem],
        out_specs=[vmem] * len(shapes),
        compiler_params=pltpu.CompilerParams(vmem_limit_bytes=8 * 1024 * 1024),
        cost_estimate=pl.CostEstimate(flops=10**7, bytes_accessed=2 * 10**6, transcendentals=0),
        name="bands",
    )(taps)
    total = summed_over(half, "sta", groups)
    narrow = total.astype(jnp.bfloat16)
    halo = []
    for shift in (2, 1, -1, -2):
        halo.append(lax.ppermute(narrow, "grid", [(i, (i + shift) % tiles) for i in range(tiles)]))
    tile = jax.ShapeDtypeStruct((CX, CY, CZ), jnp.float32)
    stacked, deblurred = pl.pallas_call(
        functools.partial(deblur_kernel, tiles),
        out_shape=(tile, tile),
        in_specs=[smem, smem] + [vmem] * (5 + len(bands)),
        out_specs=(vmem, vmem),
        compiler_params=pltpu.CompilerParams(vmem_limit_bytes=36 * 1024 * 1024),
        name="deblur",
    )(lax.axis_index("grid").astype(jnp.int32).reshape(1), spread_taps, total, *halo, *bands)
    return stacked[None], deblurred[None]


def solution(mesh):
    placed = (P(None, None, "sta"), P("grid", "sta"), P("grid", None, "sta"), P())
    return jax.shard_map(
        functools.partial(per_device, mesh.shape["sta"], mesh.shape["grid"]),
        mesh=mesh,
        in_specs=placed,
        out_specs=(P("grid", None, None, None), P("grid", None, None, None)),
        check_vma=False,
    )
```

```python
import functools
import math

import jax
import jax.numpy as jnp
from jax import lax
from jax.experimental import pallas as pl
from jax.experimental.pallas import tpu as pltpu
from jax.sharding import PartitionSpec as P

F0 = 600
NT = 6000
TAPS = 17
HALF = 8
ITERS = 4
CX = 32
CY = 8
CZ = 128
LANES = 128

TWO_PI = 2.0 * math.pi
BACKGROUND = 0.05
SMALLER = 0.25

YL, XA, XB, DC, DS, DE, DB = 0, 6, 10, 18, 22, 26, 30
ENTRIES = 38
EXTRA = 3


def sincos(t):
    u = t * t
    s = t * (1.0 + u * (-0.16666600108146667 + u * (0.008329673670232296 - u * 0.00019265798619017005)))
    c = 1.0 + u * (-0.4999999701976776 + u * (0.0416664220392704 + u * (u * 2.4071188818197697e-05 - 0.0013882155762985349)))
    return c, s


def doubled(cs):
    c, s = cs
    t = s + s
    return 1.0 - t * s, t * c


def times(p, q):
    return p[0] * q[0] - p[1] * q[1], p[0] * q[1] + p[1] * q[0]


def butterfly(values, levels):
    for level in range(levels):
        step = 1 << level
        out = list(values)
        for at in range(len(values)):
            if not at & step:
                (cr, ci), (sr, si) = values[at], values[at + step]
                out[at] = (cr - si, ci + sr)
                out[at + step] = (cr + si, ci - sr)
        values = out
    return values


def beam_kernel(chunks, own, width, scale, more, first_ref, *refs):
    x_refs, refs = refs[:chunks], refs[chunks:]
    final = scale is not None
    before = refs[0] if more else None
    out_ref, xs, *refs = refs[more:]
    tabs, refs = refs[: min(chunks, 2)], refs[min(chunks, 2) :]
    works, acc = refs[:2], (refs[2:] if final else [out_ref])
    parts = width // LANES
    for g in range(chunks):
        for b in range(own + EXTRA):
            pair = x_refs[g][b].astype(jnp.float32)
            for i in range(parts):
                xs[g, i, 2 * b : 2 * b + 2, :] = pair[:, i * LANES : (i + 1) * LANES]
    bins = (lax.broadcasted_iota(jnp.int32, (own, LANES), 0) + (first_ref[0] + F0)).astype(jnp.float32)
    half_omega = bins * (TWO_PI / NT / 2.0)
    row = lax.broadcasted_iota(jnp.int32, (8, LANES), 0)
    bits = [(row & (1 << level)) != 0 for level in range(3)]
    away = jnp.where(row < 4, 3 - row, row - 4)
    near = (away & 1) != 0, away >= 2
    sign = jnp.where(row < 4, -1.0, 1.0)
    lower = lax.broadcasted_iota(jnp.int32, (CX * CY, CZ), 1) < CZ // 2

    def tables(tab, g, i):
        def common(which):
            at = 2 * own + which
            return jnp.broadcast_to(xs[g, i, at : at + 1, :], (own, LANES))

        lag = common(0) * 64.0 + common(1)
        turns = bins * lag
        rest = turns - jnp.floor(turns * (1.0 / NT) + 0.5) * float(NT)
        turn = doubled(doubled(sincos(rest * (TWO_PI / NT / 4.0))))
        re = xs[g, i, pl.ds(0, own, stride=2), :]
        im = xs[g, i, pl.ds(1, own, stride=2), :]
        al = re * turn[0] + im * turn[1], im * turn[0] - re * turn[1]

        def put(entry, value):
            tab[i, entry * own : (entry + 1) * own, :] = value

        xl = [sincos(half_omega * common(2))]
        for _ in range(4):
            xl.append(doubled(xl[-1]))
        yl = [sincos(half_omega * common(3))]
        for _ in range(2):
            yl.append(doubled(yl[-1]))

        def products(levels):
            rows = [None]
            for level in levels:
                rows = [level[bit] if row is None else row * level[bit] for bit in range(2) for row in rows]
            return rows

        for level in range(3):
            put(YL + 2 * level, yl[level][0])
            put(YL + 2 * level + 1, yl[level][1])
        for entry, value in enumerate(products(xl[:2])):
            put(XA + entry, value)
        for entry, value in enumerate(products(xl[2:])):
            put(XB + entry, value)

        half = sincos(half_omega * common(4))
        e1 = doubled(half)
        e2 = doubled(e1)
        rows = [half, times(half, e1)]
        rows += [times(e, e2) for e in rows]
        for entry, value in enumerate(rows):
            put(DC + entry, value[0])
            put(DS + entry, value[1])
        e4 = doubled(e2)
        e8 = doubled(e4)
        for entry, value in enumerate(e4 + times(e4, e8)):
            put(DE + entry, value)
        e16 = doubled(e8)
        e48 = times(e16, doubled(e16))
        for low, high, e in ((0, 3, e48), (1, 2, e16)):
            rc, ms, mc, rs = al[0] * e[0], al[1] * e[1], al[1] * e[0], al[0] * e[1]
            put(DB + high, rc + ms)
            put(DB + 4 + high, mc - rs)
            put(DB + low, rc - ms)
            put(DB + 4 + low, mc + rs)

    def beams(tab, f):
        def spread(entry, i, rows=8):
            return jnp.broadcast_to(tab[i, pl.ds(entry * own + f, 1), :], (rows, LANES))

        def narrow(entry, i):
            return spread(entry, i, 16).astype(jnp.bfloat16)

        def pack(low, high):
            return jnp.concatenate([low, high], axis=0).astype(jnp.bfloat16)

        left, right = [], []
        for i in range(parts):
            y = None
            for level in range(3):
                level_y = jnp.where(bits[level], spread(YL + 2 * level + 1, i), spread(YL + 2 * level, i))
                y = level_y if y is None else y * level_y
            xy = [y * spread(XA + k, i) for k in range(4)]
            xy = [pack(xy[0], xy[1]), pack(xy[2], xy[3])]
            rows = []
            for b in range(8):
                by = narrow(XB + b, i)
                rows += [xy[0] * by, xy[1] * by]
            left.append(jnp.concatenate(rows, axis=0))

            def middle(entry):
                e = [spread(entry + k, i) for k in range(4)]
                return jnp.where(near[1], jnp.where(near[0], e[3], e[2]), jnp.where(near[0], e[1], e[0]))

            mc, ms = middle(DC), middle(DS) * sign
            turned = []
            for k in range(2):
                c, s = spread(DE + 2 * k, i), spread(DE + 2 * k + 1, i)
                turned.append((c * mc - s * ms, s * mc + c * ms))
            ar, ai = pack(turned[0][0], turned[1][0]), pack(turned[0][1], turned[1][1])
            na = -ai
            br = [narrow(DB + h, i) for h in range(4)]
            bi = [narrow(DB + 4 + h, i) for h in range(4)]
            rows = [ar * b for b in br] + [ar * b for b in bi] + [ai * b for b in bi] + [na * b for b in br]
            right.append(jnp.concatenate(rows, axis=0))
        return lax.dot_general(
            jnp.concatenate(left, axis=1),
            jnp.concatenate(right, axis=1),
            (((1,), (1,)), ((), ())),
            preferred_element_type=jnp.float32,
        )

    def add_power(got, work):
        above, below = got[:, :CZ] + got[:, CZ:], got[:, :CZ] - got[:, CZ:]
        reals = jnp.where(lower, above, pltpu.roll(below, CZ // 2, 1))
        imags = jnp.where(lower, pltpu.roll(above, CZ // 2, 1), below)
        values = [(reals[8 * x : 8 * x + 8], imags[8 * x : 8 * x + 8]) for x in range(CX)]
        for x, (re, im) in enumerate(butterfly(values, 5)):
            work[0, 8 * x : 8 * x + 8, :] = re
            work[1, 8 * x : 8 * x + 8, :] = im
        values = [(work[0, pl.ds(y, CX, stride=8), :], work[1, pl.ds(y, CX, stride=8), :]) for y in range(CY)]
        for y, (re, im) in enumerate(butterfly(values, 3)):
            out_ref[:, y * CZ : (y + 1) * CZ] += re * re + im * im

    batch = own
    each = parts * batch // own

    def some(n, fn):
        lax.fori_loop(0, n, lambda i, c: (fn(i), c)[1], 0)

    def both(i):
        tables(tabs[0], 0, 2 * i)
        tables(tabs[0], 0, 2 * i + 1)

    some(parts // 2, both)
    if final:
        out_ref[...] = jnp.zeros_like(out_ref)
    for g in range(chunks):
        last = g == chunks - 1
        tab = tabs[g % len(tabs)]

        def block(q, g=g, last=last, tab=tab):
            done = 0
            for j in range(batch):
                f = q * batch + j
                got = beams(tab, f)
                if g > 0:
                    got = acc[0][f] + got
                elif more:
                    got = before[f] + got
                if final and last:
                    add_power(got, works[j % 2])
                else:
                    acc[0][f] = got
                while not last and done * batch < (j + 1) * each:
                    tables(tabs[(g + 1) % 2], g + 1, q * each + done)
                    done += 1

        some(own // batch, block)

    if not final:
        return
    src = lax.broadcasted_iota(jnp.int32, (CZ, CZ), 0)
    dst = lax.broadcasted_iota(jnp.int32, (CZ, CZ), 1)
    low = src % 16
    place = (src // 16) % 4 * 32 + jnp.where(src < CZ // 2, 16 + low, 15 - low)
    swap = jnp.where(place == dst, scale, 0.0)
    blocks = [out_ref[:, y * CZ : (y + 1) * CZ] for y in range(CY)]
    natural = jnp.dot(
        jnp.concatenate(blocks, axis=0), swap, precision=lax.Precision.HIGHEST, preferred_element_type=jnp.float32
    )
    for y in range(CY):
        out_ref[:, y * CZ : (y + 1) * CZ] = natural[y * CX : (y + 1) * CX]


def beams_call(own, width, scale, at, blocks, held):
    vmem = pl.BlockSpec(memory_space=pltpu.VMEM)
    smem = pl.BlockSpec(memory_space=pltpu.SMEM)
    chunks, more, final = len(blocks), int(held is not None), scale is not None
    rows = CX * CY
    acc = (own, rows, 2 * CZ)
    scratch = [pltpu.VMEM((chunks, width // LANES, 2 * (own + EXTRA), LANES), jnp.float32)]
    scratch += [pltpu.VMEM((width // LANES, ENTRIES * own, LANES), jnp.float32)] * min(chunks, 2)
    if final:
        scratch += [pltpu.VMEM((2, rows, CZ), jnp.float32)] * 2
        scratch += [pltpu.VMEM(acc, jnp.float32)] * (chunks > 1)
    return pl.pallas_call(
        functools.partial(beam_kernel, chunks, own, width, scale, more),
        out_shape=jax.ShapeDtypeStruct((CX, CY * CZ) if final else acc, jnp.float32),
        in_specs=[smem] + [vmem] * (chunks + more),
        out_specs=vmem,
        scratch_shapes=scratch,
        compiler_params=pltpu.CompilerParams(vmem_limit_bytes=36 * 1024 * 1024),
        cost_estimate=pl.CostEstimate(
            flops=(8 if more else 0) * chunks * own * rows * CZ * width, bytes_accessed=8, transcendentals=0
        ),
        name="beams_last" if final else "beams_more" if more else "beams_own",
    )(at, *blocks, *([held] if more else []))


def split(v):
    high = v.astype(jnp.bfloat16)
    return high, (v - high.astype(jnp.float32)).astype(jnp.bfloat16)


def blur_rows():
    reach = 2 * ITERS * HALF
    sizes = [CX + 2 * (reach - HALF * blur) for blur in range(2 * ITERS + 1)]
    return list(zip(sizes[:-1], sizes[1:]))


def band_kernel(taps_ref, *refs):
    def band(axis, offset, low):
        total = jnp.zeros(offset.shape, jnp.float32)
        for tap in range(TAPS):
            total = jnp.where(offset == tap, taps_ref[axis, tap], total)
        high = total.astype(jnp.bfloat16).astype(jnp.float32)
        return jnp.where(low, total - high, high).astype(jnp.bfloat16)

    for (n, m), ref in zip(blur_rows(), refs):
        i = lax.broadcasted_iota(jnp.int32, (m, 3 * n), 0)
        p = lax.broadcasted_iota(jnp.int32, (m, 3 * n), 1)
        low = (p >= n) & (p < 2 * n)
        p = jnp.where(low, p - n, jnp.where(p >= 2 * n, p - 2 * n, p))
        ref[...] = band(0, p - i, low)
    pair = 2 * CZ
    w = lax.broadcasted_iota(jnp.int32, (pair, pair), 0)
    k = lax.broadcasted_iota(jnp.int32, (pair, pair), 1)
    offset = jnp.where(w // CZ == k // CZ, w - k + HALF, -1)
    for part in range(3):
        refs[-1][part * pair : (part + 1) * pair, :] = band(2, offset, part == 1)


def deblur_kernel(count, at_ref, taps_ref, own_ref, m2, m1, p1, p2, *refs):
    bands, (stacked_ref, est_ref) = refs[:-2], refs[-2:]
    rows = 5 * CX
    start = (at_ref[0] - 2) * CX
    x = lax.broadcasted_iota(jnp.int32, (rows, CZ), 0) + start
    inside = jnp.where((x >= 0) & (x < count * CX), 1.0, 0.0)
    outside = jnp.concatenate([1.0 - inside] * CY, axis=1)
    inside = jnp.concatenate([inside] * CY, axis=1)

    stacked = own_ref[...] * (1.0 / SMALLER) + BACKGROUND
    halo = [ref[...].astype(jnp.float32) * (1.0 / SMALLER) + BACKGROUND for ref in (m2, m1, p1, p2)]
    observed = jnp.concatenate(halo[:2] + [stacked] + halo[2:], axis=0) * inside
    for y in range(CY):
        stacked_ref[:, y, :] = stacked[:, y * CZ : (y + 1) * CZ]

    def blur(v, which):
        n = v.shape[0]
        m = n - 2 * HALF
        high, low = split(v)
        x = jnp.dot(
            bands[which][...], jnp.concatenate([high, high, low], axis=0), preferred_element_type=jnp.float32
        )
        along = []
        for j in range(CY):
            total = None
            for q in range(CY):
                term = taps_ref[1, q - j + HALF] * x[:, q * CZ : (q + 1) * CZ]
                total = term if total is None else total + term
            along.append(total)
        pairs = [jnp.concatenate(along[j : j + 2], axis=1) for j in range(0, CY, 2)]
        high, low = split(jnp.concatenate(pairs, axis=0))
        z = jnp.dot(
            jnp.concatenate([high, high, low], axis=1), bands[-1][...], preferred_element_type=jnp.float32
        )
        return jnp.concatenate([z[k * m : (k + 1) * m] for k in range(CY // 2)], axis=1)

    est, first = observed, 0
    for sweep in range(ITERS):
        blurred = blur(est, 2 * sweep)
        first += HALF
        n = blurred.shape[0]
        ratio = observed[first : first + n] / (blurred + outside[first : first + n])
        change = blur(ratio, 2 * sweep + 1)
        first += HALF
        est = est[2 * HALF : -2 * HALF] * change
    for y in range(CY):
        est_ref[:, y, :] = est[:, y * CZ : (y + 1) * CZ]


def bundle_kernel(groups, own, me_ref, spectra_ref, lag_ref, slow_ref, *refs):
    outs, (lag_in, slow_in, sems) = refs[:groups], refs[groups:]
    small = [
        pltpu.make_async_copy(lag_ref, lag_in, sems.at[groups]),
        pltpu.make_async_copy(slow_ref, slow_in, sems.at[groups + 1]),
    ]
    for copy in small:
        copy.start()
    slices = []
    for k in range(groups):
        dest = me_ref[0] ^ k if groups & (groups - 1) == 0 else lax.rem(me_ref[0] + k, groups)
        slices.append(
            pltpu.make_async_copy(spectra_ref.at[pl.ds(dest * own, own)], outs[k].at[pl.ds(0, own)], sems.at[k])
        )
        slices[k].start()
    for copy in small:
        copy.wait()
    lag = lag_in[...]
    slow = slow_in[...].astype(jnp.float32)
    pairs = [
        jnp.concatenate([(lag >> 6).astype(jnp.float32), (lag & 63).astype(jnp.float32)], axis=0),
        slow[:2],
        jnp.concatenate([slow[2:], slow[2:]], axis=0),
    ]
    for k in range(groups):
        for extra, pair in enumerate(pairs):
            outs[k][own + extra] = pair.astype(jnp.bfloat16)
    for copy in slices:
        copy.wait()


def moves(k, size):
    return [(i, i ^ k if size & (size - 1) == 0 else (i + k) % size) for i in range(size)]


def summed_over(half, axis, size):
    if size & (size - 1):
        return lax.psum(half.astype(jnp.float32), axis)
    terms = [half] + [lax.ppermute(half, axis, moves(k, size)) for k in range(1, size)]
    terms = [term.astype(jnp.float32) for term in terms]
    while len(terms) > 1:
        terms = [a + b for a, b in zip(terms[::2], terms[1::2])]
    return terms[0]


def per_device(groups, tiles, spectra, lag_samples, slowness, spread_taps):
    freqs, _, width = spectra.shape
    own = freqs // groups
    me = lax.axis_index("sta").astype(jnp.int32)
    vmem = pl.BlockSpec(memory_space=pltpu.VMEM)
    smem = pl.BlockSpec(memory_space=pltpu.SMEM)
    hbm = pl.BlockSpec(memory_space=pl.ANY)
    blocks = pl.pallas_call(
        functools.partial(bundle_kernel, groups, own),
        out_shape=[jax.ShapeDtypeStruct((own + EXTRA, 2, width), jnp.bfloat16)] * groups,
        in_specs=[smem] + [hbm] * 3,
        out_specs=[vmem] * groups,
        scratch_shapes=[
            pltpu.VMEM((1, width), jnp.int32),
            pltpu.VMEM((3, width), jnp.bfloat16),
            pltpu.SemaphoreType.DMA((groups + 2,)),
        ],
        compiler_params=pltpu.CompilerParams(vmem_limit_bytes=60 * 1024 * 1024),
        name="bundles",
    )(me.reshape(1), spectra, lag_samples, slowness[0])
    blocks = [blocks[0]] + [lax.ppermute(blocks[k], "sta", moves(k, groups)) for k in range(1, groups)]

    at = (me * own).reshape(1)
    scale = SMALLER / (freqs * width * groups)
    held = beams_call(own, width, None, at, blocks[:1], None)
    for block in blocks[1:-1]:
        held = beams_call(own, width, None, at, [block], held)
    local = beams_call(own, width, scale, at, blocks[-1:], held)

    half, taps = lax.optimization_barrier((local.astype(jnp.float16), spread_taps))
    shapes = [(m, 3 * n) for n, m in blur_rows()] + [(6 * CZ, 2 * CZ)]
    bands = pl.pallas_call(
        band_kernel,
        out_shape=[jax.ShapeDtypeStruct(shape, jnp.bfloat16) for shape in shapes],
        in_specs=[smem],
        out_specs=[vmem] * len(shapes),
        compiler_params=pltpu.CompilerParams(vmem_limit_bytes=8 * 1024 * 1024),
        cost_estimate=pl.CostEstimate(flops=10**7, bytes_accessed=2 * 10**6, transcendentals=0),
        name="bands",
    )(taps)
    total = summed_over(half, "sta", groups)
    narrow = total.astype(jnp.bfloat16)
    halo = []
    for shift in (2, 1, -1, -2):
        halo.append(lax.ppermute(narrow, "grid", [(i, (i + shift) % tiles) for i in range(tiles)]))
    tile = jax.ShapeDtypeStruct((CX, CY, CZ), jnp.float32)
    stacked, deblurred = pl.pallas_call(
        functools.partial(deblur_kernel, tiles),
        out_shape=(tile, tile),
        in_specs=[smem, smem] + [vmem] * (5 + len(bands)),
        out_specs=(vmem, vmem),
        compiler_params=pltpu.CompilerParams(vmem_limit_bytes=36 * 1024 * 1024),
        name="deblur",
    )(lax.axis_index("grid").astype(jnp.int32).reshape(1), spread_taps, total, *halo, *bands)
    return stacked[None], deblurred[None]


def solution(mesh):
    placed = (P(None, None, "sta"), P("grid", "sta"), P("grid", None, "sta"), P())
    return jax.shard_map(
        functools.partial(per_device, mesh.shape["sta"], mesh.shape["grid"]),
        mesh=mesh,
        in_specs=placed,
        out_specs=(P("grid", None, None, None), P("grid", None, None, None)),
        check_vma=False,
    )
```
